256 devices in a mesh: dp: 4 (over x_hi, core), seq: 64 (over y, x_lo, z).
Axes of the slice: x: 4 (x_hi: 2, x_lo: 2; x = x_hi * 2 + x_lo), y: 4, z: 8, core: 2. Of those that a mesh axis runs over, the one named last changes fastest.
Arguments:
- tokens: bfloat16 [4, 64, 128, 1152], P('dp', 'seq'), may hold values from -6 to 6
- modulation: float32 [4, 2, 3, 1152], P('dp'), may hold values from -3 to 3
- frame_pos: int32 [64], replicated, may hold values from 0 to 63, each once
- qkv_weight: bfloat16 [2, 1152, 1728], replicated, may hold values from -2 to 2
- out_weight: bfloat16 [2, 576, 1152], replicated, may hold values from -0.25 to 0.25
- seed_grad: bfloat16 [4, 64, 128, 1152], P('dp', None, 'seq'), may hold values from -6 to 6
Outputs:
- block_out: bfloat16 [4, 64, 128, 1152], P('dp', None, 'seq')
- tokens_grad: bfloat16 [4, 64, 128, 1152], P('dp', 'seq')
- qkv_grad: float32 [1152, 1728], P('dp', 'seq')
- proj_grad: float32 [576, 1152], P('seq', 'dp')
The draws below stay inside these ranges and needn't reach their ends.
Inputs may be any that keep to these rules, and one draw needn't show every extreme that they name: `frame_pos`: each of 0 to 63 appears once.
All inputs are finite; a program needn't handle non-finite values.
Results may differ from the reference program's by a relative error of at most 0.022.
Values may be sent and summed in bfloat16 or wider, within the bound.
No kernel may reach another device: no remote copies, remote signals or barrier semaphores. Data moves between devices by JAX's collectives and lax.ppermute only.
A program may use at most 128 MiB of HBM per device.

```python
import math
from functools import partial
import jax
import jax.numpy as jnp
from jax import lax

D = 1152
HEADS = 8
HEAD_DIM = 72
LOC = 128
HW = 576
FRAMES = 64
CLIPS = 4


def draw_qkv_weight(key, part):
    key = jax.random.fold_in(key, 7)
    first_key = jax.random.fold_in(key, 0)
    width_attn = HEADS * HEAD_DIM
    base_draw = jax.random.normal(first_key, (2, D, 3 * width_attn), jnp.float32) * D ** (-0.5)
    return base_draw.astype(jnp.bfloat16)


def level_of(rng, dims, cuts, least, high):
    def one(axis_at, shards_of):
        heights = jax.random.uniform(jax.random.fold_in(jax.random.fold_in(rng, 6), axis_at), (shards_of,), jnp.float32, least / len(cuts), high / len(cuts))
        return jnp.repeat(jnp.exp(heights), dims[axis_at] // shards_of).reshape((-1,) + (1,) * (len(dims) - axis_at - 1))

    factor_of = one(*cuts[0])
    for cut in cuts[1:]:
        factor_of = factor_of * one(*cut)
    return factor_of


def gaussian(rng, dims, width, bound, pieces=(), kind=jnp.bfloat16):
    values = jax.random.normal(rng, dims, jnp.float32) * width
    if len(pieces) > 0:
        values = level_of(rng, dims, pieces, -0.22, 0.18) * values
    return jnp.clip(values, min=-bound, max=bound).astype(kind)


def setup_inputs(seed: int = 0) -> dict:
    key_of = jax.random.split(jax.random.key(seed), 7)
    return {
        "tokens": gaussian(key_of[0], (CLIPS, FRAMES, LOC, D), 1.0, 6.0, ((0, 4), (1, 64))),
        "modulation": gaussian(key_of[1], (CLIPS, 2, 3, D), 0.5, 3.0, ((0, 4),), jnp.float32),
        "frame_pos": jax.random.permutation(key_of[2], FRAMES).astype(jnp.int32),
        "qkv_weight": draw_qkv_weight(jax.random.fold_in(key_of[6], 71), 0),
        "out_weight": gaussian(key_of[4], (2, HW, D), HW ** -0.5, 0.25),
        "seed_grad": gaussian(key_of[5], (CLIPS, FRAMES, LOC, D), 1.0, 6.0, ((0, 4), (2, 64))),
    }


EPS = 1e-06
ROPE_BASE = 10000.0

def premix(inputs, shift_row, scale_row):
    average = lax.optimization_barrier(jnp.mean(inputs, axis=-1, keepdims=True))
    centered = inputs - average
    variance = lax.optimization_barrier(jnp.mean(centered * centered, axis=-1, keepdims=True))
    normed = centered * lax.rsqrt(variance + EPS)
    return (normed * (1.0 + scale_row) + shift_row).astype(jnp.bfloat16)

def softmax_rows(scores):
    largest = lax.stop_gradient(lax.optimization_barrier(jnp.max(scores, axis=-1, keepdims=True)))
    exponent = jnp.exp(scores - largest)
    return (exponent / lax.optimization_barrier(jnp.sum(exponent, axis=-1, keepdims=True))).astype(jnp.bfloat16)

def spatial_core(query, keys, values):
    scores = jnp.einsum('cflhe,cfmhe->cfhlm', query.astype(jnp.float32), keys.astype(jnp.float32)) * HEAD_DIM ** (-0.5)
    probability = softmax_rows(scores)
    return jnp.einsum('cfhlm,cfmhe->cflhe', probability.astype(jnp.float32), values.astype(jnp.float32)).astype(jnp.bfloat16)

def rotate_half(tensor, cosines, sines):
    half_dim = tensor.shape[-1] // 2
    first = tensor[..., :half_dim]
    second = tensor[..., half_dim:]
    return jnp.concatenate([first * cosines - second * sines, second * cosines + first * sines], axis=-1)

def rope_tables(frame_pos):
    half_dim = HEAD_DIM // 2
    frequency = jnp.exp(jnp.arange(half_dim, dtype=jnp.float32) * (-2.0 * math.log(ROPE_BASE) / HEAD_DIM))
    angles = frame_pos.astype(jnp.float32)[:, None] * frequency[None, :]
    return (jnp.cos(angles)[None, :, None, None, :], jnp.sin(angles)[None, :, None, None, :])

def temporal_core(query, keys, values, cosines, sines):
    rot_query = rotate_half(query.astype(jnp.float32), cosines, sines).astype(jnp.bfloat16)
    rot_keys = rotate_half(keys.astype(jnp.float32), cosines, sines).astype(jnp.bfloat16)
    scores = jnp.einsum('cflhe,cglhe->clhfg', rot_query.astype(jnp.float32), rot_keys.astype(jnp.float32)) * HEAD_DIM ** (-0.5)
    probability = softmax_rows(scores)
    return jnp.einsum('clhfg,cglhe->cflhe', probability.astype(jnp.float32), values.astype(jnp.float32)).astype(jnp.bfloat16)

def sublayer_forward(tokens, modulate_row, qkv_weight, out_weight, attend):
    width_attn = out_weight.shape[0]
    inputs_full = tokens.astype(jnp.float32)
    shift_row = modulate_row[:, 0][:, None, None, :]
    scale_row = modulate_row[:, 1][:, None, None, :]
    gate_row = modulate_row[:, 2][:, None, None, :]
    normed, premix_back = jax.vjp(lambda inputs: premix(inputs, shift_row, scale_row), inputs_full)
    projected = jnp.dot(normed, qkv_weight, preferred_element_type=jnp.float32).astype(jnp.bfloat16)
    head_shape = projected.shape[:-1] + (HEADS, HEAD_DIM)
    query = projected[..., :width_attn].reshape(head_shape)
    keys = projected[..., width_attn:2 * width_attn].reshape(head_shape)
    values = projected[..., 2 * width_attn:].reshape(head_shape)
    attended, attend_back = jax.vjp(attend, query, keys, values)
    flat_attended = attended.reshape(projected.shape[:-1] + (width_attn,))
    branch = jnp.dot(flat_attended, out_weight, preferred_element_type=jnp.float32)
    result = (inputs_full + gate_row * branch).astype(jnp.bfloat16)
    return (result, (normed, flat_attended, gate_row, premix_back, attend_back))

def sublayer_backward(upstream, kept_state, qkv_weight, out_weight, want_weights):
    normed, flat_attended, gate_row, premix_back, attend_back = kept_state
    width_attn = out_weight.shape[0]
    width_model = out_weight.shape[1]
    contract = (((0,), (0,)), ((), ()))
    grad_full = upstream.astype(jnp.float32)
    branch_grad = (gate_row * grad_full).astype(jnp.bfloat16)
    attended_grad = jnp.dot(branch_grad, out_weight.T, preferred_element_type=jnp.float32).astype(jnp.bfloat16)
    head_shape = attended_grad.shape[:-1] + (HEADS, HEAD_DIM)
    query_grad, keys_grad, values_grad = attend_back(attended_grad.reshape(head_shape))
    flat_shape = attended_grad.shape
    projected_grad = jnp.concatenate([query_grad.reshape(flat_shape), keys_grad.reshape(flat_shape), values_grad.reshape(flat_shape)], axis=-1)
    normed_grad = jnp.dot(projected_grad, qkv_weight.T, preferred_element_type=jnp.float32).astype(jnp.bfloat16)
    inputs_grad, = premix_back(normed_grad)
    input_result = (grad_full + inputs_grad).astype(jnp.bfloat16)
    if want_weights:
        proj_part = lax.dot_general(flat_attended.reshape(-1, width_attn), branch_grad.reshape(-1, width_model), contract, preferred_element_type=jnp.float32)
        qkv_part = lax.dot_general(normed.reshape(-1, width_model), projected_grad.reshape(-1, 3 * width_attn), contract, preferred_element_type=jnp.float32)
        return (input_result, qkv_part, proj_part)
    return (input_result, None, None)

def reference(tokens, modulation, frame_pos, qkv_weight, out_weight, seed_grad):
    spatial_out, spatial_kept = sublayer_forward(tokens, modulation[:, 0], qkv_weight[0], out_weight[0], spatial_core)
    cosines, sines = rope_tables(frame_pos)
    attend_time = partial(temporal_core, cosines=cosines, sines=sines)
    block_out, temporal_kept = sublayer_forward(spatial_out, modulation[:, 1], qkv_weight[1], out_weight[1], attend_time)
    middle_grad, temporal_qkv, temporal_proj = sublayer_backward(seed_grad, temporal_kept, qkv_weight[1], out_weight[1], True)
    tokens_grad, unused_qkv, unused_proj = sublayer_backward(middle_grad, spatial_kept, qkv_weight[0], out_weight[0], False)
    return (block_out, tokens_grad, temporal_qkv, temporal_proj)
```

```python
from functools import partial
import math

import jax
import jax.numpy as jnp
import numpy as np
from jax import lax
from jax.experimental import pallas as pl
from jax.experimental.pallas import tpu as pltpu
from jax.sharding import Mesh, PartitionSpec as P

D = 1152
HEADS = 8
HEAD_DIM = 72
HALF = HEAD_DIM // 2
HW = 576
LOC = 128
FRAMES = 64
TOK = 128
SCALE = HEAD_DIM ** (-0.5)
EPS = 1e-06
ROPE_BASE = 10000.0
QKV_COLS = 27
PROJ_ROWS = 9
BLOCK = QKV_COLS + PROJ_ROWS
F32 = jnp.float32
BF16 = jnp.bfloat16

NN = (((1,), (0,)), ((), ()))
NT = (((1,), (1,)), ((), ()))
TN = (((0,), (0,)), ((), ()))


def dot(a, b, dims=NN):
    return lax.dot_general(a, b, dims, preferred_element_type=F32)


def layer_norm(x):
    centered = x - jnp.mean(x, axis=-1, keepdims=True)
    inverse = lax.rsqrt(jnp.mean(centered * centered, axis=-1, keepdims=True) + EPS)
    return centered * inverse, inverse


def layer_norm_back(grad, unit, inverse):
    first = jnp.mean(grad, axis=-1, keepdims=True)
    second = jnp.mean(grad * unit, axis=-1, keepdims=True)
    return inverse * (grad - first - unit * second)


def split_heads(x):
    lane = lax.broadcasted_iota(jnp.int32, (1, HW), 1)
    parts = []
    for h in range(HEADS):
        mine = ((lane >= h * HEAD_DIM) & (lane < (h + 1) * HEAD_DIM)).astype(F32).astype(BF16)
        parts.append(x * mine)
    return jnp.concatenate(parts, axis=0)


def head(x, h):
    return x[:, h * TOK : (h + 1) * TOK]


def rows_of(parts):
    return jnp.concatenate(parts, axis=0)


def lanes_of(parts):
    return jnp.concatenate(parts, axis=1)


def attend(query, keys_by_head, values_by_head, allowed):
    scores = dot(query, keys_by_head, NT)
    probs = []
    for h in range(HEADS):
        s = head(scores, h) * SCALE
        if allowed is not None:
            s = jnp.where(allowed, s, -1e30)
        e = jnp.exp(s - jnp.max(s, axis=-1, keepdims=True))
        probs.append((e / jnp.sum(e, axis=-1, keepdims=True)).astype(BF16))
    return probs, dot(lanes_of(probs), values_by_head).astype(BF16)


def attend_back(probs, attended_grad, query, keys_by_head, values_by_head):
    prob_grads = dot(attended_grad, values_by_head, NT)
    values_grad = dot(rows_of(probs), split_heads(attended_grad), TN)
    score_grads = []
    for h in range(HEADS):
        p = probs[h].astype(F32)
        g = head(prob_grads, h)
        s = p * (g - jnp.sum(g * p, axis=-1, keepdims=True)) * SCALE
        score_grads.append(s.astype(BF16))
    query_grad = dot(lanes_of(score_grads), keys_by_head)
    keys_grad = dot(rows_of(score_grads), split_heads(query), TN)
    return query_grad, keys_grad, values_grad


def swap_halves(x):
    lane = lax.broadcasted_iota(jnp.int32, (1, HW), 1)
    first = lax.rem(lane, HEAD_DIM) < HALF
    later = jnp.concatenate([x[:, HALF:], x[:, :HALF]], axis=1)
    earlier = jnp.concatenate([x[:, HW - HALF :], x[:, : HW - HALF]], axis=1)
    return jnp.where(first, later, earlier)


def spatial_forward_kernel(tokens, mod, qkv_w, out_w, x1, q_out, k_out, v_out, p_out):
    x = tokens[...].reshape(TOK, D).astype(F32)
    unit, _ = layer_norm(x)
    shift, scale, gate = mod[0, 0, 0:1, :], mod[0, 0, 1:2, :], mod[0, 0, 2:3, :]
    normed = (unit * (1.0 + scale) + shift).astype(BF16)
    projected = dot(normed, qkv_w[0])
    q = projected[:, :HW].astype(BF16)
    k = projected[:, HW : 2 * HW].astype(BF16)
    v = projected[:, 2 * HW :].astype(BF16)
    q_out[...] = q
    k_out[...] = k
    v_out[...] = v
    probs, attended = attend(q, split_heads(k), split_heads(v), None)
    for h in range(HEADS):
        p_out[h] = probs[h]
    branch = dot(attended, out_w[0])
    x1[...] = (x + gate * branch).astype(BF16).reshape(FRAMES, 2, D)


def spatial_backward_kernel(grad, tokens, mod, qkv_w, out_w, q_in, k_in, v_in, p_in, result):
    g = grad[...].reshape(TOK, D).astype(F32)
    unit, inverse = layer_norm(tokens[...].reshape(TOK, D).astype(F32))
    scale, gate = mod[0, 0, 1:2, :], mod[0, 0, 2:3, :]
    branch_grad = (gate * g).astype(BF16)
    attended_grad = dot(branch_grad, out_w[0], NT).astype(BF16)
    probs = [p_in[h] for h in range(HEADS)]
    grads = attend_back(probs, attended_grad, q_in[...], split_heads(k_in[...]), split_heads(v_in[...]))
    projected_grad = lanes_of(grads).astype(BF16)
    normed_grad = dot(projected_grad, qkv_w[0], NT).astype(BF16).astype(F32)
    x_grad = layer_norm_back(normed_grad * (1.0 + scale), unit, inverse)
    result[...] = (g + x_grad).astype(BF16).reshape(result.shape)


def branch_grad_kernel(seed, mod, out):
    g = seed[...].reshape(TOK, D).astype(F32)
    out[...] = (mod[0, 0, 2:3, :] * g).astype(BF16)


def temporal_kernel(
    located, seed, cosines, sines, mod, qkv_w, out_w, block_out, x_grad_out, normed_out, factors, wide
):
    x = located[...].reshape(TOK, D).astype(F32)
    unit, inverse = layer_norm(x)
    shift, scale, gate = mod[0, 0, 0:1, :], mod[0, 0, 1:2, :], mod[0, 0, 2:3, :]
    normed = (unit * (1.0 + scale) + shift).astype(BF16)
    normed_out[...] = normed
    projected = dot(normed, qkv_w[0]).astype(BF16).astype(F32)
    cos, sin = cosines[...], sines[...]

    def rotate(t):
        return (t * cos + swap_halves(t) * sin).astype(BF16)

    def rotate_back(t):
        t = t.astype(BF16).astype(F32)
        return t * cos + swap_halves(t * sin)

    q = rotate(projected[:, :HW])
    k = rotate(projected[:, HW : 2 * HW])
    v = projected[:, 2 * HW :].astype(BF16)
    keys_by_head, values_by_head = split_heads(k), split_heads(v)
    row = lax.broadcasted_iota(jnp.int32, (TOK, TOK), 0)
    column = lax.broadcasted_iota(jnp.int32, (TOK, TOK), 1)
    same = lax.rem(row, 2) == lax.rem(column, 2)
    probs, attended = attend(q, keys_by_head, values_by_head, same)
    branch = dot(attended, out_w[0])
    block_out[...] = (x + gate * branch).astype(BF16).reshape(block_out.shape)

    g = seed[...].reshape(TOK, D).astype(F32)
    branch_grad = (gate * g).astype(BF16)
    attended_grad = dot(branch_grad, out_w[0], NT).astype(BF16)
    q_grad, k_grad, v_grad = attend_back(probs, attended_grad, q, keys_by_head, values_by_head)
    grads = lanes_of([rotate_back(q_grad), rotate_back(k_grad), v_grad])
    normed_grad = dot(grads.astype(BF16), qkv_w[0], NT).astype(BF16).astype(F32)
    x_grad = layer_norm_back(normed_grad * (1.0 + scale), unit, inverse)
    x_grad_out[...] = (g + x_grad).astype(BF16).reshape(FRAMES, 2, D)

    wide[: 3 * HW, :] = grads.T
    wide[3 * HW :, :] = attended.astype(F32).T
    for z in range(8):
        parts = [wide[pl.ds((g * 8 + z) * QKV_COLS, QKV_COLS), :] for g in range(8)]
        parts += [wide[pl.ds(3 * HW + (g * 8 + z) * PROJ_ROWS, PROJ_ROWS), :] for g in range(8)]
        factors[z] = jnp.concatenate(parts, axis=0).astype(BF16)


def weight_grad_kernel(core, normed, branch_grad, factors, keep, send):
    left = lanes_of([factors[z] for z in range(8)])
    qkv = dot(left[: 8 * QKV_COLS], normed[...])
    proj = dot(left[8 * QKV_COLS :], branch_grad[...])
    width = D // 4
    first = core[0] == 0
    for x in range(2):
        for g in range(8):
            rows = jnp.concatenate(
                [qkv[g * QKV_COLS : (g + 1) * QKV_COLS], proj[g * PROJ_ROWS : (g + 1) * PROJ_ROWS]], axis=0
            )
            a = rows[:, (2 * x) * width : (2 * x + 1) * width]
            b = rows[:, (2 * x + 1) * width : (2 * x + 2) * width]
            keep[x * 8 + g] = jnp.where(first, a, b)
            send[x * 8 + g] = jnp.where(first, b, a).astype(BF16)


def vmem(n):
    return [pl.BlockSpec(memory_space=pltpu.VMEM)] * n


def sub(s):
    return [
        pl.BlockSpec((1, 1, 3, D), lambda i: (0, s, 0, 0)),
        pl.BlockSpec((1, D, 3 * HW), lambda i: (s, 0, 0)),
        pl.BlockSpec((1, HW, D), lambda i: (s, 0, 0)),
    ]


def whole(*shape):
    return pl.BlockSpec(shape, lambda i: (0,) * len(shape))


def params(mib):
    return pltpu.CompilerParams(vmem_limit_bytes=mib * 2**20)


def shards(tokens, modulation, frame_pos, qkv_weight, out_weight, seed_grad):
    shape = jax.ShapeDtypeStruct
    seed = seed_grad.reshape(FRAMES, 2, D)
    tokens = tokens.reshape(TOK, D)

    branch_grad = pl.pallas_call(
        branch_grad_kernel,
        grid=(1,),
        out_shape=shape((TOK, D), BF16),
        in_specs=[whole(FRAMES, 2, D), sub(1)[0]],
        out_specs=whole(TOK, D),
        compiler_params=params(16),
        name="branch_grad",
    )(seed, modulation)
    branch_all = lax.all_gather(branch_grad, "z", tiled=True)

    x1, q, k, v, p = pl.pallas_call(
        spatial_forward_kernel,
        grid=(1,),
        out_shape=(
            shape((FRAMES, 2, D), BF16),
            shape((TOK, HW), BF16),
            shape((TOK, HW), BF16),
            shape((TOK, HW), BF16),
            shape((HEADS, TOK, TOK), BF16),
        ),
        in_specs=[whole(TOK, D), *sub(0)],
        out_specs=(whole(FRAMES, 2, D), whole(TOK, HW), whole(TOK, HW), whole(TOK, HW), whole(HEADS, TOK, TOK)),
        compiler_params=params(40),
        name="spatial_forward",
    )(tokens, modulation, qkv_weight, out_weight)

    seq = ("y", "xl", "z")
    located = lax.all_to_all(x1, seq, split_axis=0, concat_axis=0, tiled=True)

    frequency = jnp.exp(jnp.arange(HALF, dtype=F32) * (-2.0 * math.log(ROPE_BASE) / HEAD_DIM))
    lane_frequency = jnp.tile(frequency, 2 * HEADS)
    angles = jnp.repeat(frame_pos.astype(F32), 2)[:, None] * lane_frequency[None, :]
    sign = np.tile(np.repeat(np.array([-1.0, 1.0], np.float32), HALF), HEADS)
    cosines = jnp.cos(angles)
    sines = jnp.sin(angles) * sign[None, :]

    block_out, located_grad, normed, factors = pl.pallas_call(
        temporal_kernel,
        grid=(1,),
        out_shape=(
            shape((FRAMES, 2, D), BF16),
            shape((FRAMES, 2, D), BF16),
            shape((TOK, D), BF16),
            shape((8, 8 * BLOCK, TOK), BF16),
        ),
        in_specs=[whole(FRAMES, 2, D), whole(FRAMES, 2, D), whole(TOK, HW), whole(TOK, HW), *sub(1)],
        out_specs=(whole(FRAMES, 2, D), whole(FRAMES, 2, D), whole(TOK, D), whole(8, 8 * BLOCK, TOK)),
        scratch_shapes=[pltpu.VMEM((4 * HW, TOK), F32)],
        compiler_params=params(48),
        name="temporal",
    )(located, seed, cosines, sines, modulation, qkv_weight, out_weight)

    normed_all = lax.all_gather(normed, "z", tiled=True)
    framed_grad = lax.all_to_all(located_grad, seq, split_axis=0, concat_axis=0, tiled=True)

    tokens_grad = pl.pallas_call(
        spatial_backward_kernel,
        grid=(1,),
        out_shape=shape((TOK, D), BF16),
        in_specs=[
            whole(FRAMES, 2, D),
            whole(TOK, D),
            *sub(0),
            whole(TOK, HW),
            whole(TOK, HW),
            whole(TOK, HW),
            whole(HEADS, TOK, TOK),
        ],
        out_specs=whole(TOK, D),
        compiler_params=params(48),
        name="spatial_backward",
    )(framed_grad, tokens, modulation, qkv_weight, out_weight, q, k, v, p)

    factors = lax.all_to_all(factors, "z", split_axis=0, concat_axis=0, tiled=True)
    core = lax.axis_index("core").reshape(1).astype(jnp.int32)
    keep, send = pl.pallas_call(
        weight_grad_kernel,
        out_shape=(shape((16, BLOCK, D // 4), F32), shape((16, BLOCK, D // 4), BF16)),
        in_specs=[pl.BlockSpec(memory_space=pltpu.SMEM), *vmem(3)],
        out_specs=tuple(vmem(2)),
        compiler_params=params(40),
        name="weight_grad",
    )(core, normed_all, branch_all, factors)
    received = lax.ppermute(send, "core", [(0, 1), (1, 0)])
    both = (keep + received.astype(F32)).astype(BF16)
    parts = lax.all_to_all(both, ("xh", "y", "xl"), split_axis=0, concat_axis=0, tiled=True)
    total = jnp.sum(parts.astype(F32), axis=0)
    return (
        block_out.reshape(1, FRAMES, 2, D),
        tokens_grad.reshape(1, 1, LOC, D),
        total[:QKV_COLS].T,
        total[QKV_COLS:],
    )


def solution(mesh):
    sizes = (2, 2, 4, 2, 8)
    split = Mesh(mesh.devices.reshape(sizes), ("xh", "core", "y", "xl", "z"))
    dp, seq = ("xh", "core"), ("y", "xl", "z")
    return jax.shard_map(
        shards,
        mesh=split,
        in_specs=(
            P(dp, seq, None, None),
            P(dp, None, None, None),
            P(),
            P(),
            P(),
            P(dp, None, seq, None),
        ),
        out_specs=(
            P(dp, None, seq, None),
            P(dp, seq, None, None),
            P(dp, seq),
            P(seq, dp),
        ),
        check_vma=False,
    )
```

```python
from functools import partial
import math

import jax
import jax.numpy as jnp
import numpy as np
from jax import lax
from jax.experimental import pallas as pl
from jax.experimental.pallas import tpu as pltpu
from jax.sharding import Mesh, PartitionSpec as P

D = 1152
HEADS = 8
HEAD_DIM = 72
HALF = HEAD_DIM // 2
HW = 576
LOC = 128
FRAMES = 64
TOK = 128
SCALE = HEAD_DIM ** (-0.5)
EPS = 1e-06
ROPE_BASE = 10000.0
QKV_COLS = 27
PROJ_ROWS = 9
BLOCK = 40
Y = 4
PARTS = 16
WIDTH = D // 4
F32 = jnp.float32
BF16 = jnp.bfloat16

NN = (((1,), (0,)), ((), ()))
NT = (((1,), (1,)), ((), ()))
TN = (((0,), (0,)), ((), ()))


def dot(a, b, dims=NN):
    return lax.dot_general(a, b, dims, preferred_element_type=F32)


def layer_norm(x):
    centered = x - jnp.mean(x, axis=-1, keepdims=True)
    inverse = lax.rsqrt(jnp.mean(centered * centered, axis=-1, keepdims=True) + EPS)
    return centered * inverse, inverse


def layer_norm_back(grad, unit, inverse):
    first = jnp.mean(grad, axis=-1, keepdims=True)
    second = jnp.mean(grad * unit, axis=-1, keepdims=True)
    return inverse * (grad - first - unit * second)


def split_heads(x):
    lane = lax.broadcasted_iota(jnp.int32, (1, HW), 1)
    parts = []
    for h in range(HEADS):
        mine = ((lane >= h * HEAD_DIM) & (lane < (h + 1) * HEAD_DIM)).astype(F32).astype(BF16)
        parts.append(x * mine)
    return jnp.concatenate(parts, axis=0)


def head(x, h):
    return x[:, h * TOK : (h + 1) * TOK]


def rows_of(parts):
    return jnp.concatenate(parts, axis=0)


def lanes_of(parts):
    return jnp.concatenate(parts, axis=1)


def attend(query, keys_by_head, values_by_head, allowed):
    scores = dot(query, keys_by_head, NT)
    probs = []
    for h in range(HEADS):
        s = head(scores, h) * SCALE
        if allowed is not None:
            s = jnp.where(allowed, s, -1e30)
        e = jnp.exp(s - jnp.max(s, axis=-1, keepdims=True))
        probs.append((e / jnp.sum(e, axis=-1, keepdims=True)).astype(BF16))
    return probs, dot(lanes_of(probs), values_by_head).astype(BF16)


def attend_back(probs, attended_grad, query, keys_by_head, values_by_head):
    prob_grads = dot(attended_grad, values_by_head, NT)
    values_grad = dot(rows_of(probs), split_heads(attended_grad), TN)
    score_grads = []
    for h in range(HEADS):
        p = probs[h].astype(F32)
        g = head(prob_grads, h)
        s = p * (g - jnp.sum(g * p, axis=-1, keepdims=True)) * SCALE
        score_grads.append(s.astype(BF16))
    query_grad = dot(lanes_of(score_grads), keys_by_head)
    keys_grad = dot(rows_of(score_grads), split_heads(query), TN)
    return query_grad, keys_grad, values_grad


def swap_halves(x):
    lane = lax.broadcasted_iota(jnp.int32, (1, HW), 1)
    first = lax.rem(lane, HEAD_DIM) < HALF
    later = jnp.concatenate([x[:, HALF:], x[:, :HALF]], axis=1)
    earlier = jnp.concatenate([x[:, HW - HALF :], x[:, : HW - HALF]], axis=1)
    return jnp.where(first, later, earlier)


def fetch(pairs, sems):
    copies = [pltpu.make_async_copy(src, dst, sems.at[i]) for i, (src, dst) in enumerate(pairs)]
    for c in copies:
        c.start()
    return copies


def store(pairs, sems):
    return fetch(pairs, sems)


def wait_all(copies):
    for c in copies:
        c.wait()


def regroup(x):
    main = [x[:, d * WIDTH : d * WIDTH + 256] for d in range(4)]
    tail = [x[:, d * WIDTH + 256 : (d + 1) * WIDTH] for d in range(4)]
    return jnp.concatenate(main + tail, axis=1)


def branch_grad_kernel(seed, mod, out):
    g = seed[...].reshape(TOK, D).astype(F32)
    out[...] = regroup((mod[0, 2, 1:2, :] * g).astype(BF16))


def temporal_normed_kernel(located, mod, out):
    unit, _ = layer_norm(located[...].reshape(TOK, D).astype(F32))
    out[...] = regroup((unit * (1.0 + mod[0, 1, 1:2, :]) + mod[0, 0, 1:2, :]).astype(BF16))


def spatial_forward_kernel(
    tokens, mod, qkv_w, out_w, x1, q_out, k_out, v_out, p_out,
    tokens_v, mod_v, w_v, o_v, x1_v, q_v, k_v, v_v, p_v, in_sem, out_sem,
):
    copies = fetch(
        [(tokens, tokens_v), (mod, mod_v)]
        + [(qkv_w.at[0, pl.ds(i * HW, HW)], w_v.at[pl.ds(i * HW, HW)]) for i in range(3)]
        + [(out_w.at[0], o_v)],
        in_sem,
    )
    wait_all(copies[:2])
    x = tokens_v[...].astype(F32)
    unit, _ = layer_norm(x)
    shift, scale, gate = mod_v[0, 0, 0:1, :], mod_v[0, 1, 0:1, :], mod_v[0, 2, 0:1, :]
    normed = (unit * (1.0 + scale) + shift).astype(BF16)
    parts = []
    for i, out in enumerate((q_v, k_v, v_v)):
        copies[2 + i].wait()
        part = dot(normed, w_v[i * HW : (i + 1) * HW, :], NT).astype(BF16)
        out[...] = part
        parts.append(part)
    q, k, v = parts
    saves = store([(q_v, q_out), (k_v, k_out), (v_v, v_out)], out_sem)
    probs, attended = attend(q, split_heads(k), split_heads(v), None)
    for h in range(HEADS):
        p_v[h] = probs[h]
    save_p = pltpu.make_async_copy(p_v, p_out, out_sem.at[3])
    save_p.start()
    copies[5].wait()
    branch = dot(attended, o_v[...])
    x1_v[...] = (x + gate * branch).astype(BF16).reshape(FRAMES, 2, D)
    save_x = pltpu.make_async_copy(x1_v, x1, out_sem.at[4])
    save_x.start()
    wait_all(saves + [save_p, save_x])


def spatial_attention_back_kernel(
    grad, mod, out_w, q_in, k_in, v_in, p_in, result,
    grad_v, mod_v, o_v, q_v, k_v, v_v, p_v, result_v, in_sem, out_sem,
):
    copies = fetch(
        [(grad, grad_v), (mod, mod_v), (out_w.at[0], o_v), (v_in, v_v), (p_in, p_v), (k_in, k_v), (q_in, q_v)], in_sem
    )
    wait_all(copies)
    g = grad_v[...].reshape(TOK, D).astype(F32)
    branch_grad = (mod_v[0, 2, 0:1, :] * g).astype(BF16)
    attended_grad = dot(branch_grad, o_v[...], NT).astype(BF16)
    probs = [p_v[h] for h in range(HEADS)]
    grads = attend_back(probs, attended_grad, q_v[...], split_heads(k_v[...]), split_heads(v_v[...]))
    result_v[...] = lanes_of(grads).astype(BF16)
    save = pltpu.make_async_copy(result_v, result, out_sem)
    save.start()
    save.wait()


def spatial_input_back_kernel(
    grad, tokens, mod, qkv_w, projected_grad, result,
    grad_v, tokens_v, mod_v, w_v, p_v, result_v, in_sem, out_sem,
):
    copies = fetch([(projected_grad, p_v), (qkv_w.at[0], w_v), (tokens, tokens_v), (mod, mod_v), (grad, grad_v)], in_sem)
    wait_all(copies)
    g = grad_v[...].reshape(TOK, D).astype(F32)
    unit, inverse = layer_norm(tokens_v[...].astype(F32))
    normed_grad = dot(p_v[...], w_v[...]).astype(BF16).astype(F32)
    x_grad = layer_norm_back(normed_grad * (1.0 + mod_v[0, 1, 0:1, :]), unit, inverse)
    result_v[...] = (g + x_grad).astype(BF16)
    save = pltpu.make_async_copy(result_v, result, out_sem)
    save.start()
    save.wait()


def temporal_kernel(
    located, seed, cosines, sines, mod, qkv_w, out_w, block_out, x_grad_out, factors,
    located_v, seed_v, cos_v, sin_v, mod_v, w_v, o_v, block_v, x_grad_v, factors_v, wide, in_sem, out_sem,
):
    copies = fetch(
        [(located, located_v), (mod, mod_v)]
        + [(qkv_w.at[1, pl.ds(i * HW, HW)], w_v.at[pl.ds(i * HW, HW)]) for i in range(3)]
        + [(cosines, cos_v), (sines, sin_v), (out_w.at[1], o_v), (seed, seed_v)],
        in_sem,
    )
    wait_all(copies[:2])
    x = located_v[...].reshape(TOK, D).astype(F32)
    unit, inverse = layer_norm(x)
    shift, scale, gate = mod_v[0, 0, 1:2, :], mod_v[0, 1, 1:2, :], mod_v[0, 2, 1:2, :]
    normed = (unit * (1.0 + scale) + shift).astype(BF16)
    parts = []
    for i in range(3):
        copies[2 + i].wait()
        parts.append(dot(normed, w_v[i * HW : (i + 1) * HW, :], NT).astype(BF16))
    wait_all(copies[5:7])
    cos, sin = cos_v[...], sin_v[...]

    def rotate(t):
        t = t.astype(F32)
        return (t * cos + swap_halves(t) * sin).astype(BF16)

    def rotate_back(t):
        t = t.astype(BF16).astype(F32)
        return t * cos + swap_halves(t * sin)

    q, k, v = rotate(parts[0]), rotate(parts[1]), parts[2]
    keys_by_head, values_by_head = split_heads(k), split_heads(v)
    row = lax.broadcasted_iota(jnp.int32, (TOK, TOK), 0)
    column = lax.broadcasted_iota(jnp.int32, (TOK, TOK), 1)
    same = lax.rem(row, 2) == lax.rem(column, 2)
    probs, attended = attend(q, keys_by_head, values_by_head, same)
    copies[7].wait()
    branch = dot(attended, o_v[...])
    block_v[...] = (x + gate * branch).astype(BF16).reshape(FRAMES, 2, D)
    save_block = pltpu.make_async_copy(block_v, block_out, out_sem.at[0])
    save_block.start()

    copies[8].wait()
    g = seed_v[...].reshape(TOK, D).astype(F32)
    branch_grad = (gate * g).astype(BF16)
    attended_grad = dot(branch_grad, o_v[...], NT).astype(BF16)
    q_grad, k_grad, v_grad = attend_back(probs, attended_grad, q, keys_by_head, values_by_head)
    grads = lanes_of([rotate_back(q_grad), rotate_back(k_grad), v_grad])

    wide[: 3 * HW, :] = grads.T
    wide[3 * HW :, :] = attended.astype(F32).T
    empty = jnp.zeros((BLOCK - QKV_COLS - PROJ_ROWS, TOK), F32)
    for y in range(Y):
        pieces = []
        for s in range(PARTS):
            i = y * PARTS + s
            pieces += [
                wide[pl.ds(i * QKV_COLS, QKV_COLS), :],
                wide[pl.ds(3 * HW + i * PROJ_ROWS, PROJ_ROWS), :],
                empty,
            ]
        factors_v[y] = jnp.concatenate(pieces, axis=0).astype(BF16)
    save_factors = pltpu.make_async_copy(factors_v, factors, out_sem.at[1])
    save_factors.start()

    normed_grad = dot(grads.astype(BF16), w_v[...]).astype(BF16).astype(F32)
    x_grad = layer_norm_back(normed_grad * (1.0 + scale), unit, inverse)
    x_grad_v[...] = (g + x_grad).astype(BF16).reshape(FRAMES, 2, D)
    save_grad = pltpu.make_async_copy(x_grad_v, x_grad_out, out_sem.at[2])
    save_grad.start()
    wait_all([save_block, save_factors, save_grad])


def weight_grad_kernel(core, normed, branch_grad, factors, keep, send, n_v, b_v, f_v, in_sem):
    copies = fetch([(normed, n_v), (factors, f_v), (branch_grad, b_v)], in_sem)
    wait_all(copies)
    left = lanes_of([f_v[y] for y in range(Y)])
    is_qkv = lax.rem(lax.broadcasted_iota(jnp.int32, (PARTS * BLOCK, 1), 0), BLOCK) < QKV_COLS
    sums = jnp.where(is_qkv, dot(left, n_v[...]), dot(left, b_v[...]))
    first = core[0] == 0

    def quarter(d):
        main = sums[:, d * 256 : (d + 1) * 256]
        tail = sums[:, 1024 + d * 32 : 1024 + (d + 1) * 32]
        return main.reshape(2, 8, BLOCK, 256), tail.reshape(2, 8, BLOCK, 32)

    for x in range(2):
        for half, (a, b) in enumerate(zip(quarter(2 * x), quarter(2 * x + 1), strict=True)):
            lanes = slice(0, 256) if half == 0 else slice(256, WIDTH)
            keep[:, x, :, :, lanes] = jnp.where(first, a, b).astype(BF16)
            send[:, x, :, :, lanes] = jnp.where(first, b, a).astype(BF16)


def add_cores_kernel(xl, keep, received, mine, send):
    own, other = xl[0], 1 - xl[0]
    mine[...] = (keep[own].astype(F32) + received[own].astype(F32)).astype(BF16)
    send[...] = (keep[other].astype(F32) + received[other].astype(F32)).astype(BF16)


def hbm(n):
    return [pl.BlockSpec(memory_space=pltpu.HBM)] * n


def vmem(n):
    return [pl.BlockSpec(memory_space=pltpu.VMEM)] * n


def whole(*shape):
    return pl.BlockSpec(shape, lambda i: (0,) * len(shape))


def params(mib):
    return pltpu.CompilerParams(vmem_limit_bytes=mib * 2**20)


def out(dtype, *shape):
    return pltpu.HBM(shape, dtype)


def buf(dtype, *shape):
    return pltpu.VMEM(shape, dtype)


def dma(*n):
    return pltpu.SemaphoreType.DMA(n) if n else pltpu.SemaphoreType.DMA


PAIRS = (FRAMES, 2, D)
MOD = (1, 3, 2, D)
QKV_W = (3 * HW, D)
OUT_W = (HW, D)
ATT = (TOK, HW)
PROB = (HEADS, TOK, TOK)
CHUNK = (BLOCK, WIDTH)


def shards(tokens, modulation, frame_pos, qkv_weight, out_weight, seed_grad):
    seed = seed_grad.reshape(PAIRS)
    tokens = tokens.reshape(TOK, D)
    mod = modulation.transpose(0, 2, 1, 3)
    qkv_w = qkv_weight.swapaxes(1, 2)

    branch_grad = pl.pallas_call(
        branch_grad_kernel,
        grid=(1,),
        out_shape=out(BF16, TOK, D),
        in_specs=[whole(*PAIRS), whole(*MOD)],
        out_specs=whole(TOK, D),
        compiler_params=params(16),
        name="branch_grad",
    )(seed, mod)
    branch_all = lax.all_gather(branch_grad, "y", tiled=True)

    x1, q, k, v, p = pl.pallas_call(
        spatial_forward_kernel,
        out_shape=(out(BF16, *PAIRS), out(BF16, *ATT), out(BF16, *ATT), out(BF16, *ATT), out(BF16, *PROB)),
        in_specs=hbm(4),
        out_specs=tuple(hbm(5)),
        scratch_shapes=[
            buf(BF16, TOK, D), buf(F32, *MOD), buf(BF16, *QKV_W), buf(BF16, *OUT_W), buf(BF16, *PAIRS),
            buf(BF16, *ATT), buf(BF16, *ATT), buf(BF16, *ATT), buf(BF16, *PROB), dma(6), dma(5),
        ],
        compiler_params=params(40),
        name="spatial_forward",
    )(tokens, mod, qkv_w, out_weight)

    seq = ("y", "xl", "z")
    located = lax.all_to_all(x1, seq, split_axis=0, concat_axis=0, tiled=True)

    frequency = jnp.exp(jnp.arange(HALF, dtype=F32) * (-2.0 * math.log(ROPE_BASE) / HEAD_DIM))
    lane_frequency = jnp.tile(frequency, 2 * HEADS)
    angles = jnp.repeat(frame_pos.astype(F32), 2)[:, None] * lane_frequency[None, :]
    sign = np.tile(np.repeat(np.array([-1.0, 1.0], np.float32), HALF), HEADS)
    cosines = jnp.cos(angles)
    sines = jnp.sin(angles) * sign[None, :]

    normed = pl.pallas_call(
        temporal_normed_kernel,
        grid=(1,),
        out_shape=out(BF16, TOK, D),
        in_specs=[whole(*PAIRS), whole(*MOD)],
        out_specs=whole(TOK, D),
        compiler_params=params(16),
        name="temporal_normed",
    )(located, mod)
    normed_all = lax.all_gather(normed, "y", tiled=True)

    block_out, located_grad, factors = pl.pallas_call(
        temporal_kernel,
        out_shape=(out(BF16, *PAIRS), out(BF16, *PAIRS), out(BF16, Y, PARTS * BLOCK, TOK)),
        in_specs=hbm(7),
        out_specs=tuple(hbm(3)),
        scratch_shapes=[
            buf(BF16, *PAIRS), buf(BF16, *PAIRS), buf(F32, *ATT), buf(F32, *ATT), buf(F32, *MOD),
            buf(BF16, *QKV_W), buf(BF16, *OUT_W), buf(BF16, *PAIRS), buf(BF16, *PAIRS),
            buf(BF16, Y, PARTS * BLOCK, TOK), buf(F32, 4 * HW, TOK), dma(9), dma(3),
        ],
        compiler_params=params(48),
        name="temporal",
    )(located, seed, cosines, sines, mod, qkv_w, out_weight)

    factors = lax.all_to_all(factors, "y", split_axis=0, concat_axis=0, tiled=True)
    framed_grad = lax.all_to_all(located_grad, seq, split_axis=0, concat_axis=0, tiled=True)

    core = lax.axis_index("core").reshape(1).astype(jnp.int32)
    keep, send = pl.pallas_call(
        weight_grad_kernel,
        out_shape=(out(BF16, 2, 2, 8, *CHUNK), out(BF16, 2, 2, 8, *CHUNK)),
        grid=(1,),
        in_specs=[pl.BlockSpec(memory_space=pltpu.SMEM), *hbm(3)],
        out_specs=(whole(2, 2, 8, *CHUNK), whole(2, 2, 8, *CHUNK)),
        scratch_shapes=[buf(BF16, Y * TOK, D), buf(BF16, Y * TOK, D), buf(BF16, Y, PARTS * BLOCK, TOK), dma(3)],
        compiler_params=params(48),
        name="weight_grad",
    )(core, normed_all, branch_all, factors)
    received = lax.ppermute(send, "core", [(0, 1), (1, 0)])

    projected_grad = pl.pallas_call(
        spatial_attention_back_kernel,
        out_shape=out(BF16, TOK, 3 * HW),
        in_specs=hbm(7),
        out_specs=hbm(1)[0],
        scratch_shapes=[
            buf(BF16, *PAIRS), buf(F32, *MOD), buf(BF16, *OUT_W), buf(BF16, *ATT), buf(BF16, *ATT), buf(BF16, *ATT),
            buf(BF16, *PROB), buf(BF16, TOK, 3 * HW), dma(7), dma(),
        ],
        compiler_params=params(40),
        name="spatial_attention_back",
    )(framed_grad, mod, out_weight, q, k, v, p)

    xl = lax.axis_index("xl").reshape(1).astype(jnp.int32)
    mine, send = pl.pallas_call(
        add_cores_kernel,
        grid=(1,),
        out_shape=(out(BF16, 2, 8, *CHUNK), out(BF16, 2, 8, *CHUNK)),
        in_specs=[pl.BlockSpec(memory_space=pltpu.SMEM), whole(2, 2, 8, *CHUNK), whole(2, 2, 8, *CHUNK)],
        out_specs=(whole(2, 8, *CHUNK), whole(2, 8, *CHUNK)),
        compiler_params=params(24),
        name="add_cores",
    )(xl, keep, received)
    received = lax.ppermute(send, "xl", [(0, 1), (1, 0)])

    tokens_grad = pl.pallas_call(
        spatial_input_back_kernel,
        out_shape=out(BF16, TOK, D),
        in_specs=hbm(5),
        out_specs=hbm(1)[0],
        scratch_shapes=[
            buf(BF16, *PAIRS), buf(BF16, TOK, D), buf(F32, *MOD), buf(BF16, *QKV_W), buf(BF16, TOK, 3 * HW),
            buf(BF16, TOK, D), dma(5), dma(),
        ],
        compiler_params=params(32),
        name="spatial_input_back",
    )(framed_grad, tokens, mod, qkv_w, projected_grad)

    both = (mine.astype(F32) + received.astype(F32)).astype(BF16).reshape(16, *CHUNK)
    parts = lax.all_to_all(both, ("xh", "z"), split_axis=0, concat_axis=0, tiled=True)
    total = jnp.sum(parts.astype(F32), axis=0)
    return (
        block_out.reshape(1, FRAMES, 2, D),
        tokens_grad.reshape(1, 1, LOC, D),
        total[:QKV_COLS].T,
        total[QKV_COLS : QKV_COLS + PROJ_ROWS],
    )


def solution(mesh):
    sizes = (2, 2, 4, 2, 8)
    split = Mesh(mesh.devices.reshape(sizes), ("xh", "core", "y", "xl", "z"))
    dp, seq = ("xh", "core"), ("y", "xl", "z")
    return jax.shard_map(
        shards,
        mesh=split,
        in_specs=(
            P(dp, seq, None, None),
            P(dp, None, None, None),
            P(),
            P(),
            P(),
            P(dp, None, seq, None),
        ),
        out_specs=(
            P(dp, None, seq, None),
            P(dp, seq, None, None),
            P(dp, seq),
            P(seq, dp),
        ),
        check_vma=False,
    )
```

```python
from functools import partial
import math

import jax
import jax.numpy as jnp
import numpy as np
from jax import lax
from jax.experimental import pallas as pl
from jax.experimental.pallas import tpu as pltpu
from jax.sharding import Mesh, PartitionSpec as P

D = 1152
HEADS = 8
HEAD_DIM = 72
HALF = HEAD_DIM // 2
HW = 576
LOC = 128
FRAMES = 64
TOK = 128
SCALE = HEAD_DIM ** (-0.5)
EPS = 1e-06
ROPE_BASE = 10000.0
QKV_COLS = 27
PROJ_ROWS = 9
BLOCK = 40
Y = 4
PARTS = 16
WIDTH = D // 4
F32 = jnp.float32
BF16 = jnp.bfloat16

NN = (((1,), (0,)), ((), ()))
NT = (((1,), (1,)), ((), ()))
TN = (((0,), (0,)), ((), ()))


def dot(a, b, dims=NN):
    return lax.dot_general(a, b, dims, preferred_element_type=F32)


def layer_norm(x):
    centered = x - jnp.mean(x, axis=-1, keepdims=True)
    inverse = lax.rsqrt(jnp.mean(centered * centered, axis=-1, keepdims=True) + EPS)
    return centered * inverse, inverse


def layer_norm_back(grad, unit, inverse):
    first = jnp.mean(grad, axis=-1, keepdims=True)
    second = jnp.mean(grad * unit, axis=-1, keepdims=True)
    return inverse * (grad - first - unit * second)


def split_heads(x):
    lane = lax.broadcasted_iota(jnp.int32, (1, HW), 1)
    parts = []
    for h in range(HEADS):
        mine = ((lane >= h * HEAD_DIM) & (lane < (h + 1) * HEAD_DIM)).astype(F32).astype(BF16)
        parts.append(x * mine)
    return jnp.concatenate(parts, axis=0)


def head(x, h):
    return x[:, h * TOK : (h + 1) * TOK]


def rows_of(parts):
    return jnp.concatenate(parts, axis=0)


def lanes_of(parts):
    return jnp.concatenate(parts, axis=1)


def attend(query, keys_by_head, values_by_head, allowed):
    scores = dot(query, keys_by_head, NT)
    probs = []
    for h in range(HEADS):
        s = head(scores, h) * SCALE
        if allowed is not None:
            s = jnp.where(allowed, s, -1e30)
        e = jnp.exp(s - jnp.max(s, axis=-1, keepdims=True))
        probs.append((e / jnp.sum(e, axis=-1, keepdims=True)).astype(BF16))
    return probs, dot(lanes_of(probs), values_by_head).astype(BF16)


def attend_back(probs, attended_grad, query, keys_by_head, values_by_head):
    prob_grads = dot(attended_grad, values_by_head, NT)
    values_grad = dot(rows_of(probs), split_heads(attended_grad), TN)
    score_grads = []
    for h in range(HEADS):
        p = probs[h].astype(F32)
        g = head(prob_grads, h)
        s = p * (g - jnp.sum(g * p, axis=-1, keepdims=True)) * SCALE
        score_grads.append(s.astype(BF16))
    query_grad = dot(lanes_of(score_grads), keys_by_head)
    keys_grad = dot(rows_of(score_grads), split_heads(query), TN)
    return query_grad, keys_grad, values_grad


def swap_halves(x):
    lane = lax.broadcasted_iota(jnp.int32, (1, HW), 1)
    first = lax.rem(lane, HEAD_DIM) < HALF
    later = jnp.concatenate([x[:, HALF:], x[:, :HALF]], axis=1)
    earlier = jnp.concatenate([x[:, HW - HALF :], x[:, : HW - HALF]], axis=1)
    return jnp.where(first, later, earlier)


def fetch(pairs, sems):
    copies = [pltpu.make_async_copy(src, dst, sems.at[i]) for i, (src, dst) in enumerate(pairs)]
    for c in copies:
        c.start()
    return copies


def store(pairs, sems):
    return fetch(pairs, sems)


def wait_all(copies):
    for c in copies:
        c.wait()


def regroup(x):
    main = [x[:, d * WIDTH : d * WIDTH + 256] for d in range(4)]
    tail = [x[:, d * WIDTH + 256 : (d + 1) * WIDTH] for d in range(4)]
    return jnp.concatenate(main + tail, axis=1)


def branch_grad_kernel(seed, mod, sent, kept, seed_v, sent_v, kept_v, sems):
    (load,) = fetch([(seed, seed_v)], sems.at[pl.ds(0, 1)])
    load.wait()
    g = seed_v[...].reshape(TOK, D).astype(F32)
    branch_grad = (mod[0, 2, 1:2, :] * g).astype(BF16)
    sent_v[...] = regroup(branch_grad)
    kept_v[...] = branch_grad
    wait_all(fetch([(sent_v, sent), (kept_v, kept)], sems.at[pl.ds(1, 2)]))


def rope_tables(pos):
    row = lax.broadcasted_iota(jnp.int32, (TOK, FRAMES), 0)
    frame = lax.broadcasted_iota(jnp.int32, (TOK, FRAMES), 1)
    mine = (row >= 2 * frame) & (row < 2 * frame + 2)
    time = jnp.sum(jnp.where(mine, pos.astype(F32), 0.0), axis=-1, keepdims=True)
    lane = lax.broadcasted_iota(jnp.int32, (1, HW), 1)
    frequency = jnp.exp(lax.rem(lane, HALF).astype(F32) * (-2.0 * math.log(ROPE_BASE) / HEAD_DIM))
    angles = time * frequency
    sign = jnp.where(lax.rem(lane, HEAD_DIM) < HALF, -1.0, 1.0)
    return jnp.cos(angles), jnp.sin(angles) * sign


def tables_kernel(pos, cos_out, sin_out, cos_v, sin_v, sems):
    cos_v[...], sin_v[...] = rope_tables(pos[...])
    wait_all(fetch([(cos_v, cos_out), (sin_v, sin_out)], sems))


def spatial_forward_kernel(
    place, tokens, mod, qkv_w, out_w, x1, q_out, k_out, v_out, p_out,
    tokens_v, mod_v, w_v, o_v, normed_v, x1_v, q_v, k_v, v_v, p_v, in_sem, out_sem,
):
    copies = fetch(
        [(tokens, tokens_v), (mod, mod_v)]
        + [(qkv_w.at[0, pl.ds(i * HW, HW)], w_v.at[pl.ds(i * HW, HW)]) for i in range(3)]
        + [(out_w.at[0], o_v)],
        in_sem,
    )
    wait_all(copies[:2])

    @pl.when(place[0] >= 0)
    def _():
        unit, _ = layer_norm(tokens_v[...].astype(F32))
        normed_v[...] = (unit * (1.0 + mod_v[0, 1, 0:1, :]) + mod_v[0, 0, 0:1, :]).astype(BF16)

    for i, held in enumerate((q_v, k_v, v_v)):
        copies[2 + i].wait()

        @pl.when(place[0] >= 0)
        def _(i=i, held=held):
            held[...] = dot(normed_v[...], w_v[i * HW : (i + 1) * HW, :], NT).astype(BF16)

    probs, attended = attend(q_v[...], split_heads(k_v[...]), split_heads(v_v[...]), None)
    for h in range(HEADS):
        p_v[h] = probs[h]
    saves = fetch([(q_v, q_out), (k_v, k_out), (v_v, v_out), (p_v, p_out)], out_sem.at[pl.ds(0, 4)])
    copies[5].wait()
    branch = dot(attended, o_v[...])
    x1_v[...] = (tokens_v[...].astype(F32) + mod_v[0, 2, 0:1, :] * branch).astype(BF16).reshape(FRAMES, 2, D)
    saves += fetch([(x1_v, x1)], out_sem.at[pl.ds(4, 1)])
    wait_all(saves)


def spatial_attention_back_kernel(
    grad, mod, out_w, q_in, k_in, v_in, p_in, result, o_v, q_v, k_v, v_v, p_v, sems
):
    copies = fetch([(out_w.at[0], o_v), (v_in, v_v), (p_in, p_v), (k_in, k_v), (q_in, q_v)], sems)
    g = grad[...].reshape(TOK, D).astype(F32)
    branch_grad = (mod[0, 2, 0:1, :] * g).astype(BF16)
    wait_all(copies)
    attended_grad = dot(branch_grad, o_v[...], NT).astype(BF16)
    probs = [p_v[h] for h in range(HEADS)]
    grads = attend_back(probs, attended_grad, q_v[...], split_heads(k_v[...]), split_heads(v_v[...]))
    result[...] = lanes_of(grads).astype(BF16)


def spatial_input_back_kernel(grad, tokens, mod, qkv_w, projected_grad, result, tokens_v, w_v, result_v, sems):
    copies = fetch([(tokens, tokens_v), (qkv_w.at[0], w_v)], sems.at[pl.ds(0, 2)])
    copies[0].wait()
    g = grad[...].reshape(TOK, D).astype(F32)
    unit, inverse = layer_norm(tokens_v[...].astype(F32))
    copies[1].wait()
    normed_grad = dot(projected_grad[...], w_v[...]).astype(BF16).astype(F32)
    x_grad = layer_norm_back(normed_grad * (1.0 + mod[0, 1, 0:1, :]), unit, inverse)
    result_v[...] = (g + x_grad).astype(BF16)
    wait_all(fetch([(result_v, result)], sems.at[pl.ds(2, 1)]))


def temporal_attention_kernel(
    place, located, mod, cosines, sines, qkv_w, out_w, branch_grad,
    attended_out, projected_grad, unit_out, inverse_out, w_out, sent, own, to_1, to_2, to_3,
    branch_v, o_v, cos_v, sin_v, sent_v, normed_v, qkv_v, factors_v, wide, in_sems, sems, factor_sems,
):
    copies = fetch(
        [(qkv_w.at[1, pl.ds(i * HW, HW)], w_out.at[pl.ds(i * HW, HW)]) for i in range(3)]
        + [(cosines, cos_v), (sines, sin_v), (out_w.at[1], o_v), (branch_grad, branch_v)],
        in_sems,
    )
    @pl.when(place[0] >= 0)
    def _():
        unit, inverse = layer_norm(located[...].reshape(TOK, D).astype(F32))
        unit_out[...] = unit
        inverse_out[...] = jnp.broadcast_to(inverse, (TOK, TOK))
        normed = (unit * (1.0 + mod[0, 1, 1:2, :]) + mod[0, 0, 1:2, :]).astype(BF16)
        normed_v[...] = normed
        sent_v[...] = regroup(normed)

    saves = fetch([(sent_v, sent)], sems)
    for i in range(3):
        copies[i].wait()

        @pl.when(place[0] >= 0)
        def _(i=i):
            qkv_v[i] = dot(normed_v[...], w_out[i * HW : (i + 1) * HW, :], NT).astype(BF16)

    parts = [qkv_v[i] for i in range(3)]
    wait_all(copies[3:5])
    cos, sin = cos_v[...], sin_v[...]

    def rotate(t):
        t = t.astype(F32)
        return (t * cos + swap_halves(t) * sin).astype(BF16)

    def rotate_back(t):
        t = t.astype(BF16).astype(F32)
        return t * cos + swap_halves(t * sin)

    q, k, v = rotate(parts[0]), rotate(parts[1]), parts[2]
    keys_by_head, values_by_head = split_heads(k), split_heads(v)
    row = lax.broadcasted_iota(jnp.int32, (TOK, TOK), 0)
    column = lax.broadcasted_iota(jnp.int32, (TOK, TOK), 1)
    same = lax.rem(row, 2) == lax.rem(column, 2)
    probs, attended = attend(q, keys_by_head, values_by_head, same)
    attended_out[...] = attended
    wait_all(copies[5:])
    attended_grad = dot(branch_v[...], o_v[...], NT).astype(BF16)
    q_grad, k_grad, v_grad = attend_back(probs, attended_grad, q, keys_by_head, values_by_head)
    grads = lanes_of([rotate_back(q_grad), rotate_back(k_grad), v_grad])
    projected_grad[...] = grads.astype(BF16)

    wide[: 3 * HW, :] = grads.T
    wide[3 * HW :, :] = attended.astype(F32).T
    empty = jnp.zeros((BLOCK - QKV_COLS - PROJ_ROWS, TOK), F32)
    for y in range(Y):
        pieces = []
        for s in range(PARTS):
            i = y * PARTS + s
            pieces += [
                wide[pl.ds(i * QKV_COLS, QKV_COLS), :],
                wide[pl.ds(3 * HW + i * PROJ_ROWS, PROJ_ROWS), :],
                empty,
            ]
        factors_v[y] = jnp.concatenate(pieces, axis=0).astype(BF16)
    saves += fetch(
        [(factors_v.at[lax.rem(place[0] + k, Y)], ref) for k, ref in enumerate((own, to_1, to_2, to_3))], factor_sems
    )
    wait_all(saves)


def temporal_input_back_kernel(projected_grad, qkv_w, seed, mod, unit, inverse, result, result_v, sem):
    g = seed[...].reshape(TOK, D).astype(F32)
    normed_grad = dot(projected_grad[...], qkv_w[...]).astype(BF16).astype(F32)
    x_grad = layer_norm_back(normed_grad * (1.0 + mod[0, 1, 1:2, :]), unit[...], inverse[:, 0:1])
    result_v[...] = (g + x_grad).astype(BF16).reshape(FRAMES, 2, D)
    save = pltpu.make_async_copy(result_v, result, sem)
    save.start()
    save.wait()


def block_out_kernel(attended, out_w, located, mod, result, o_v, located_v, result_v, sems):
    copies = fetch([(out_w.at[1], o_v), (located, located_v)], sems.at[pl.ds(0, 2)])
    wait_all(copies)
    x = located_v[...].reshape(TOK, D).astype(F32)
    branch = dot(attended[...], o_v[...])
    result_v[...] = (x + mod[0, 2, 1:2, :] * branch).astype(BF16).reshape(FRAMES, 2, D)
    wait_all(fetch([(result_v, result)], sems.at[pl.ds(2, 1)]))


def weight_grad_kernel(core, *refs):
    normed, branch_grad, factors = refs[0:Y], refs[Y : 2 * Y], refs[2 * Y : 3 * Y]
    keep, send, keep_v, send_v, sems = refs[3 * Y :]
    left = lanes_of([f[...] for f in factors])
    is_qkv = lax.rem(lax.broadcasted_iota(jnp.int32, (PARTS * BLOCK, 1), 0), BLOCK) < QKV_COLS
    from_normed = dot(left, rows_of([n[...] for n in normed]))
    from_branch = dot(left, rows_of([n[...] for n in branch_grad]))
    sums = jnp.where(is_qkv, from_normed, from_branch)
    tails = sums[:, 1024:].reshape(PARTS, 5, 8, TOK)
    first = core[0] == 0
    copies = []

    def chunk(d):
        main = [sums[:, d * 256 + i * TOK : d * 256 + (i + 1) * TOK].reshape(PARTS, BLOCK, TOK) for i in range(2)]
        packed = jnp.concatenate([tails[:, i, :, d * 32 : (d + 1) * 32] for i in range(4)], axis=-1)
        last = tails[:, 4]
        if d > 0:
            last = jnp.concatenate([last[:, :, d * 32 :], last[:, :, : d * 32]], axis=-1)
        return jnp.concatenate(main + [packed, last], axis=1)

    for x in range(2):
        a, b = chunk(2 * x), chunk(2 * x + 1)
        send_v[x] = jnp.where(first, b, a).astype(BF16)
        keep_v[x] = jnp.where(first, a, b).astype(BF16)
        copies += fetch([(send_v.at[x], send.at[x]), (keep_v.at[x], keep.at[x])], sems.at[x])
    wait_all(copies)


def add_kernel(a, b, result, result_v, sems):
    copies = []
    for i in range(2):
        result_v[i] = (a[i].astype(F32) + b[i].astype(F32)).astype(BF16)
        copies.append(pltpu.make_async_copy(result_v.at[i], result.at[i], sems.at[i]))
        copies[i].start()
    wait_all(copies)


def sum_kernel(parts, qkv, proj, qkv_v, proj_v, sems):
    total = parts[0].astype(F32)
    for i in range(1, 2 * PARTS):
        total = total + parts[i].astype(F32)
    packed, last = total[2 * BLOCK : 2 * BLOCK + 8], total[2 * BLOCK + 8 :]
    tail = jnp.concatenate([packed[:, i * 32 : (i + 1) * 32] for i in range(4)] + [last[:, :32]], axis=0)
    full = jnp.concatenate([total[:BLOCK], total[BLOCK : 2 * BLOCK], tail], axis=1)
    qkv_v[...] = full[:QKV_COLS]
    proj_v[...] = full[QKV_COLS : QKV_COLS + PROJ_ROWS]
    wait_all(fetch([(qkv_v, qkv), (proj_v, proj)], sems))


def call(kernel, name, inputs, outputs, scratch=(), mib=24, us=2.0):
    return pl.pallas_call(
        kernel,
        out_shape=tuple(space(shape, dtype) for space, dtype, shape in outputs),
        in_specs=[pl.BlockSpec(memory_space=space) for space, _ in inputs],
        out_specs=tuple(pl.BlockSpec(memory_space=space) for space, _, _ in outputs),
        scratch_shapes=list(scratch),
        compiler_params=pltpu.CompilerParams(vmem_limit_bytes=mib * 2**20),
        cost_estimate=pl.CostEstimate(flops=int(us * 1e9), bytes_accessed=int(us * 3e6), transcendentals=0),
        name=name,
    )(*[pltpu.with_memory_space_constraint(x, space) if space is not pltpu.SMEM else x for space, x in inputs])


def over(axis, size, k, x):
    return lax.ppermute(x, axis, [(i, (i + k) % size) for i in range(size)])


def hbm(n):
    return [pl.BlockSpec(memory_space=pltpu.HBM)] * n


def vmem(n):
    return [pl.BlockSpec(memory_space=pltpu.VMEM)] * n


def whole(*shape):
    return pl.BlockSpec(shape, lambda i: (0,) * len(shape))


def params(mib):
    return pltpu.CompilerParams(vmem_limit_bytes=mib * 2**20)


def out(dtype, *shape):
    return pltpu.HBM(shape, dtype)


def buf(dtype, *shape):
    return pltpu.VMEM(shape, dtype)


def dma(*n):
    return pltpu.SemaphoreType.DMA(n) if n else pltpu.SemaphoreType.DMA


HBM, VMEM, SMEM = pltpu.HBM, pltpu.VMEM, pltpu.SMEM
PAIRS = (FRAMES, 2, D)
MOD = (1, 3, 2, D)
QKV_W = (3 * HW, D)
OUT_W = (HW, D)
ATT = (TOK, HW)
PROB = (HEADS, TOK, TOK)
CHUNK = (96, TOK)
FACTOR = (PARTS * BLOCK, TOK)


def shards(tokens, modulation, frame_pos, qkv_weight, out_weight, seed_grad):
    seed = seed_grad.reshape(PAIRS)
    tokens = tokens.reshape(TOK, D)
    mod = modulation.transpose(0, 2, 1, 3)
    qkv_w = qkv_weight.swapaxes(1, 2)
    seq = ("y", "xl", "z")

    place = lax.axis_index("y").reshape(1).astype(jnp.int32)
    x1, q, k, v, p = call(
        spatial_forward_kernel,
        "spatial_forward",
        [(SMEM, place), (HBM, tokens), (HBM, mod), (HBM, qkv_w), (HBM, out_weight)],
        [(HBM, BF16, PAIRS), (HBM, BF16, ATT), (HBM, BF16, ATT), (HBM, BF16, ATT), (HBM, BF16, PROB)],
        [
            buf(BF16, TOK, D), buf(F32, *MOD), buf(BF16, *QKV_W), buf(BF16, *OUT_W), buf(BF16, TOK, D),
            buf(BF16, *PAIRS), buf(BF16, *ATT), buf(BF16, *ATT), buf(BF16, *ATT), buf(BF16, *PROB), dma(6), dma(5),
        ],
        us=5.0,
    )
    located = lax.all_to_all(x1, seq, split_axis=0, concat_axis=0, tiled=True)

    later_seed, later_pos, _ = lax.optimization_barrier((seed, frame_pos, x1))
    sent, branch_grad = call(
        branch_grad_kernel,
        "branch_grad",
        [(HBM, later_seed), (VMEM, mod)],
        [(HBM, BF16, (TOK, D)), (HBM, BF16, (TOK, D))],
        [buf(BF16, *PAIRS), buf(BF16, TOK, D), buf(BF16, TOK, D), dma(3)],
        us=2.0,
    )
    branch_all = [sent] + [over("y", Y, i, sent) for i in range(1, Y)]

    cosines, sines = call(
        tables_kernel,
        "tables",
        [(VMEM, later_pos.reshape(1, FRAMES))],
        [(HBM, F32, ATT), (HBM, F32, ATT)],
        [buf(F32, *ATT), buf(F32, *ATT), dma(2)],
        us=1.5,
    )
    located, branch_grad, cosines = lax.optimization_barrier((located, branch_grad, cosines))
    attended, projected_grad, unit, inverse, w1, normed, *factors = call(
        temporal_attention_kernel,
        "temporal_attention",
        [
            (SMEM, place), (VMEM, located), (VMEM, mod), (HBM, cosines), (HBM, sines), (HBM, qkv_w), (HBM, out_weight),
            (HBM, branch_grad),
        ],
        [
            (VMEM, BF16, ATT), (VMEM, BF16, (TOK, 3 * HW)), (VMEM, F32, (TOK, D)), (VMEM, F32, (TOK, TOK)),
            (VMEM, BF16, QKV_W), (HBM, BF16, (TOK, D)),
        ]
        + [(HBM, BF16, FACTOR)] * Y,
        [
            buf(BF16, TOK, D), buf(BF16, *OUT_W), buf(F32, *ATT), buf(F32, *ATT), buf(BF16, TOK, D),
            buf(BF16, TOK, D), buf(BF16, 3, *ATT), buf(BF16, Y, *FACTOR), buf(F32, 4 * HW, TOK), dma(7), dma(1), dma(Y),
        ],
        us=7.0,
    )
    normed_all = [normed] + [over("y", Y, i, normed) for i in range(1, Y)]
    factors = [factors[0]] + [over("y", Y, i, factors[i]) for i in range(1, Y)]
    (located_grad,) = call(
        temporal_input_back_kernel,
        "temporal_input_back",
        [(VMEM, projected_grad), (VMEM, w1), (VMEM, seed), (VMEM, mod), (VMEM, unit), (VMEM, inverse)],
        [(HBM, BF16, PAIRS)],
        [buf(BF16, *PAIRS), dma()],
        us=3.0,
    )
    framed_grad = lax.all_to_all(located_grad, seq, split_axis=0, concat_axis=0, tiled=True)

    core = lax.axis_index("core").reshape(1).astype(jnp.int32)
    keep, send = call(
        weight_grad_kernel,
        "weight_grad",
        [(SMEM, core)] + [(VMEM, x) for x in (*normed_all, *branch_all, *factors)],
        [(HBM, BF16, (2, PARTS, *CHUNK)), (HBM, BF16, (2, PARTS, *CHUNK))],
        [buf(BF16, 2, PARTS, *CHUNK), buf(BF16, 2, PARTS, *CHUNK), dma(2, 2)],
        us=4.6,
    )
    framed_grad, send = lax.optimization_barrier((framed_grad, send))
    received = lax.ppermute(send, "core", [(0, 1), (1, 0)])

    (halves,) = call(
        add_kernel,
        "add_cores",
        [(VMEM, keep), (VMEM, received)],
        [(HBM, BF16, (2, PARTS, *CHUNK))],
        [buf(BF16, 2, PARTS, *CHUNK), dma(2)],
        us=1.0,
    )
    parts = lax.all_to_all(
        halves.reshape(2 * PARTS, *CHUNK), ("xh", "xl", "z"), split_axis=0, concat_axis=0, tiled=True
    )

    framed_grad, attended, _ = lax.optimization_barrier((framed_grad, attended, halves))
    (projected_grad,) = call(
        spatial_attention_back_kernel,
        "spatial_attention_back",
        [(VMEM, framed_grad), (VMEM, mod), (HBM, out_weight), (HBM, q), (HBM, k), (HBM, v), (HBM, p)],
        [(VMEM, BF16, (TOK, 3 * HW))],
        [buf(BF16, *OUT_W), buf(BF16, *ATT), buf(BF16, *ATT), buf(BF16, *ATT), buf(BF16, *PROB), dma(5)],
        us=3.5,
    )
    (tokens_grad,) = call(
        spatial_input_back_kernel,
        "spatial_input_back",
        [(VMEM, framed_grad), (HBM, tokens), (VMEM, mod), (HBM, qkv_w), (VMEM, projected_grad)],
        [(HBM, BF16, (TOK, D))],
        [buf(BF16, TOK, D), buf(BF16, *QKV_W), buf(BF16, TOK, D), dma(3)],
        us=3.0,
    )
    (block_out,) = call(
        block_out_kernel,
        "block_out",
        [(VMEM, attended), (HBM, out_weight), (HBM, located), (VMEM, mod)],
        [(HBM, BF16, PAIRS)],
        [buf(BF16, *OUT_W), buf(BF16, *PAIRS), buf(BF16, *PAIRS), dma(3)],
        us=2.0,
    )
    qkv_grad, proj_grad = call(
        sum_kernel,
        "sum_parts",
        [(VMEM, parts)],
        [(HBM, F32, (QKV_COLS, WIDTH)), (HBM, F32, (PROJ_ROWS, WIDTH))],
        [buf(F32, QKV_COLS, WIDTH), buf(F32, PROJ_ROWS, WIDTH), dma(2)],
        us=1.5,
    )
    return (
        block_out.reshape(1, FRAMES, 2, D),
        tokens_grad.reshape(1, 1, LOC, D),
        qkv_grad.T,
        proj_grad,
    )


def solution(mesh):
    sizes = (2, 2, 4, 2, 8)
    split = Mesh(mesh.devices.reshape(sizes), ("xh", "core", "y", "xl", "z"))
    dp, seq = ("xh", "core"), ("y", "xl", "z")
    return jax.shard_map(
        shards,
        mesh=split,
        in_specs=(
            P(dp, seq, None, None),
            P(dp, None, None, None),
            P(),
            P(),
            P(),
            P(dp, None, seq, None),
        ),
        out_specs=(
            P(dp, None, seq, None),
            P(dp, seq, None, None),
            P(dp, seq),
            P(seq, dp),
        ),
        check_vma=False,
    )
```

```python
from functools import partial
import math

import jax
import jax.numpy as jnp
import numpy as np
from jax import lax
from jax.experimental import pallas as pl
from jax.experimental.pallas import tpu as pltpu
from jax.sharding import Mesh, PartitionSpec as P

D = 1152
HEADS = 8
HEAD_DIM = 72
HALF = HEAD_DIM // 2
HW = 576
LOC = 128
FRAMES = 64
TOK = 128
SCALE = HEAD_DIM ** (-0.5)
EPS = 1e-06
ROPE_BASE = 10000.0
QKV_COLS = 27
PROJ_ROWS = 9
BLOCK = 40
Y = 4
PARTS = 16
WIDTH = D // 4
F32 = jnp.float32
BF16 = jnp.bfloat16

NN = (((1,), (0,)), ((), ()))
NT = (((1,), (1,)), ((), ()))
TN = (((0,), (0,)), ((), ()))


def dot(a, b, dims=NN):
    return lax.dot_general(a, b, dims, preferred_element_type=F32)


def layer_norm(x):
    centered = x - jnp.mean(x, axis=-1, keepdims=True)
    inverse = lax.rsqrt(jnp.mean(centered * centered, axis=-1, keepdims=True) + EPS)
    return centered * inverse, inverse


def layer_norm_back(grad, unit, inverse):
    first = jnp.mean(grad, axis=-1, keepdims=True)
    second = jnp.mean(grad * unit, axis=-1, keepdims=True)
    return inverse * (grad - first - unit * second)


def split_heads(x):
    lane = lax.broadcasted_iota(jnp.int32, (1, HW), 1)
    parts = []
    for h in range(HEADS):
        mine = ((lane >= h * HEAD_DIM) & (lane < (h + 1) * HEAD_DIM)).astype(F32).astype(BF16)
        parts.append(x * mine)
    return jnp.concatenate(parts, axis=0)


def head(x, h):
    return x[:, h * TOK : (h + 1) * TOK]


def rows_of(parts):
    return jnp.concatenate(parts, axis=0)


def lanes_of(parts):
    return jnp.concatenate(parts, axis=1)


def attend(query, keys_by_head, values_by_head, allowed):
    scores = dot(query, keys_by_head, NT)
    probs = []
    for h in range(HEADS):
        s = head(scores, h) * SCALE
        if allowed is not None:
            s = jnp.where(allowed, s, -1e30)
        e = jnp.exp(s - jnp.max(s, axis=-1, keepdims=True))
        probs.append((e / jnp.sum(e, axis=-1, keepdims=True)).astype(BF16))
    return probs, dot(lanes_of(probs), values_by_head).astype(BF16)


def attend_back(probs, attended_grad, query, keys_by_head, values_by_head):
    prob_grads = dot(attended_grad, values_by_head, NT)
    values_grad = dot(rows_of(probs), split_heads(attended_grad), TN)
    score_grads = []
    for h in range(HEADS):
        p = probs[h].astype(F32)
        g = head(prob_grads, h)
        s = p * (g - jnp.sum(g * p, axis=-1, keepdims=True)) * SCALE
        score_grads.append(s.astype(BF16))
    query_grad = dot(lanes_of(score_grads), keys_by_head)
    keys_grad = dot(rows_of(score_grads), split_heads(query), TN)
    return query_grad, keys_grad, values_grad


def swap_halves(x):
    lane = lax.broadcasted_iota(jnp.int32, (1, HW), 1)
    first = lax.rem(lane, HEAD_DIM) < HALF
    later = jnp.concatenate([x[:, HALF:], x[:, :HALF]], axis=1)
    earlier = jnp.concatenate([x[:, HW - HALF :], x[:, : HW - HALF]], axis=1)
    return jnp.where(first, later, earlier)


def fetch(pairs, sems):
    copies = [pltpu.make_async_copy(src, dst, sems.at[i]) for i, (src, dst) in enumerate(pairs)]
    for c in copies:
        c.start()
    return copies


def store(pairs, sems):
    return fetch(pairs, sems)


def start_all(copies):
    for c in copies:
        c.start()


def wait_all(copies):
    for c in copies:
        c.wait()


def regroup(x):
    main = [x[:, d * WIDTH : d * WIDTH + 256] for d in range(4)]
    tail = [x[:, d * WIDTH + 256 : (d + 1) * WIDTH] for d in range(4)]
    return jnp.concatenate(main + tail, axis=1)


def branch_grad_kernel(seed, mod, sent, kept, seed_v, sent_v, kept_v, sems):
    (load,) = fetch([(seed, seed_v)], sems.at[pl.ds(0, 1)])
    load.wait()
    g = seed_v[...].reshape(TOK, D).astype(F32)
    branch_grad = (mod[0, 2, 1:2, :] * g).astype(BF16)
    sent_v[...] = regroup(branch_grad)
    kept_v[...] = branch_grad
    wait_all(fetch([(sent_v, sent), (kept_v, kept)], sems.at[pl.ds(1, 2)]))


def rope_tables(pos):
    row = lax.broadcasted_iota(jnp.int32, (TOK, FRAMES), 0)
    frame = lax.broadcasted_iota(jnp.int32, (TOK, FRAMES), 1)
    mine = (row >= 2 * frame) & (row < 2 * frame + 2)
    time = jnp.sum(jnp.where(mine, pos.astype(F32), 0.0), axis=-1, keepdims=True)
    lane = lax.broadcasted_iota(jnp.int32, (1, HW), 1)
    frequency = jnp.exp(lax.rem(lane, HALF).astype(F32) * (-2.0 * math.log(ROPE_BASE) / HEAD_DIM))
    angles = time * frequency
    sign = jnp.where(lax.rem(lane, HEAD_DIM) < HALF, -1.0, 1.0)
    return jnp.cos(angles), jnp.sin(angles) * sign


def tables_kernel(pos, cos_out, sin_out, cos_v, sin_v, sems):
    cos_v[...], sin_v[...] = rope_tables(pos[...])
    wait_all(fetch([(cos_v, cos_out), (sin_v, sin_out)], sems))


def spatial_forward_kernel(
    place, tokens, mod, qkv_w, out_w, x1, q_out, k_out, v_out, p_out,
    tokens_v, mod_v, w_v, o_v, normed_v, x1_v, q_v, k_v, v_v, p_v, in_sem, out_sem,
):
    pairs = [(tokens, tokens_v), (mod, mod_v)]
    pairs += [(qkv_w.at[0, pl.ds(i * HW, HW)], w_v.at[pl.ds(i * HW, HW)]) for i in range(3)] + [(out_w.at[0], o_v)]
    copies = [pltpu.make_async_copy(src, dst, in_sem.at[i]) for i, (src, dst) in enumerate(pairs)]
    start_all(copies)
    wait_all(copies[:2])

    @pl.when(place[0] >= 0)
    def _():
        unit, _ = layer_norm(tokens_v[...].astype(F32))
        normed_v[...] = (unit * (1.0 + mod_v[0, 1, 0:1, :]) + mod_v[0, 0, 0:1, :]).astype(BF16)

    for i, held in enumerate((q_v, k_v, v_v)):
        copies[2 + i].wait()

        @pl.when(place[0] >= 0)
        def _(i=i, held=held):
            held[...] = dot(normed_v[...], w_v[i * HW : (i + 1) * HW, :], NT).astype(BF16)

    probs, attended = attend(q_v[...], split_heads(k_v[...]), split_heads(v_v[...]), None)
    for h in range(HEADS):
        p_v[h] = probs[h]
    saves = fetch([(q_v, q_out), (k_v, k_out), (v_v, v_out), (p_v, p_out)], out_sem.at[pl.ds(0, 4)])
    copies[5].wait()
    branch = dot(attended, o_v[...])
    x1_v[...] = (tokens_v[...].astype(F32) + mod_v[0, 2, 0:1, :] * branch).astype(BF16).reshape(FRAMES, 2, D)
    saves += fetch([(x1_v, x1)], out_sem.at[pl.ds(4, 1)])
    wait_all(saves)


def spatial_attention_back_kernel(
    grad, mod, out_w, q_in, k_in, v_in, p_in, result, o_v, q_v, k_v, v_v, p_v, sems
):
    copies = fetch([(out_w.at[0], o_v), (v_in, v_v), (p_in, p_v), (k_in, k_v), (q_in, q_v)], sems)
    g = grad[...].reshape(TOK, D).astype(F32)
    branch_grad = (mod[0, 2, 0:1, :] * g).astype(BF16)
    wait_all(copies)
    attended_grad = dot(branch_grad, o_v[...], NT).astype(BF16)
    probs = [p_v[h] for h in range(HEADS)]
    grads = attend_back(probs, attended_grad, q_v[...], split_heads(k_v[...]), split_heads(v_v[...]))
    result[...] = lanes_of(grads).astype(BF16)


def spatial_input_back_kernel(grad, tokens, mod, qkv_w, projected_grad, result, tokens_v, w_v, result_v, sems):
    copies = fetch([(tokens, tokens_v), (qkv_w.at[0], w_v)], sems.at[pl.ds(0, 2)])
    copies[0].wait()
    g = grad[...].reshape(TOK, D).astype(F32)
    unit, inverse = layer_norm(tokens_v[...].astype(F32))
    copies[1].wait()
    normed_grad = dot(projected_grad[...], w_v[...]).astype(BF16).astype(F32)
    x_grad = layer_norm_back(normed_grad * (1.0 + mod[0, 1, 0:1, :]), unit, inverse)
    result_v[...] = (g + x_grad).astype(BF16)
    wait_all(fetch([(result_v, result)], sems.at[pl.ds(2, 1)]))


def temporal_attention_kernel(
    place, located, mod, cosines, sines, qkv_w, out_w, branch_grad,
    attended_out, projected_grad, unit_out, inverse_out, w_out, own, to_1, to_2, to_3,
    branch_v, o_v, cos_v, sin_v, sent_v, normed_v, qkv_v, factors_v, wide, in_sems, sems, factor_sems,
):
    pairs = [(qkv_w.at[1, pl.ds(i * HW, HW)], w_out.at[pl.ds(i * HW, HW)]) for i in range(3)]
    pairs += [(cosines, cos_v), (sines, sin_v), (out_w.at[1], o_v), (branch_grad, branch_v)]
    copies = [pltpu.make_async_copy(src, dst, in_sems.at[i]) for i, (src, dst) in enumerate(pairs)]
    start_all(copies)
    @pl.when(place[0] >= 0)
    def _():
        unit, inverse = layer_norm(located[...].reshape(TOK, D).astype(F32))
        unit_out[...] = unit
        inverse_out[...] = jnp.broadcast_to(inverse, (TOK, TOK))
        normed = (unit * (1.0 + mod[0, 1, 1:2, :]) + mod[0, 0, 1:2, :]).astype(BF16)
        normed_v[...] = normed
        grouped = regroup(normed)
        sent_v[...] = rows_of([grouped[:, t * TOK : (t + 1) * TOK] for t in range(D // TOK)])

    messages = (own, to_1, to_2, to_3)
    saves = fetch([(sent_v, ref.at[pl.ds(FACTOR[0], D)]) for ref in messages], sems)
    for i in range(3):
        copies[i].wait()

        @pl.when(place[0] >= 0)
        def _(i=i):
            qkv_v[i] = dot(normed_v[...], w_out[i * HW : (i + 1) * HW, :], NT).astype(BF16)

    parts = [qkv_v[i] for i in range(3)]
    wait_all(copies[3:5])
    cos, sin = cos_v[...], sin_v[...]

    def rotate(t):
        t = t.astype(F32)
        return (t * cos + swap_halves(t) * sin).astype(BF16)

    def rotate_back(t):
        t = t.astype(BF16).astype(F32)
        return t * cos + swap_halves(t * sin)

    q, k, v = rotate(parts[0]), rotate(parts[1]), parts[2]
    keys_by_head, values_by_head = split_heads(k), split_heads(v)
    row = lax.broadcasted_iota(jnp.int32, (TOK, TOK), 0)
    column = lax.broadcasted_iota(jnp.int32, (TOK, TOK), 1)
    same = lax.rem(row, 2) == lax.rem(column, 2)
    probs, attended = attend(q, keys_by_head, values_by_head, same)
    attended_out[...] = attended
    wait_all(copies[5:])
    attended_grad = dot(branch_v[...], o_v[...], NT).astype(BF16)
    q_grad, k_grad, v_grad = attend_back(probs, attended_grad, q, keys_by_head, values_by_head)
    grads = lanes_of([rotate_back(q_grad), rotate_back(k_grad), v_grad])
    projected_grad[...] = grads.astype(BF16)

    wide[: 3 * HW, :] = grads.T
    wide[3 * HW :, :] = attended.astype(F32).T
    empty = jnp.zeros((BLOCK - QKV_COLS - PROJ_ROWS, TOK), F32)
    for y in range(Y):
        pieces = []
        for s in range(PARTS):
            i = y * PARTS + s
            pieces += [
                wide[pl.ds(i * QKV_COLS, QKV_COLS), :],
                wide[pl.ds(3 * HW + i * PROJ_ROWS, PROJ_ROWS), :],
                empty,
            ]
        factors_v[y] = jnp.concatenate(pieces, axis=0).astype(BF16)
    saves += fetch(
        [(factors_v.at[lax.rem(place[0] + k, Y)], ref.at[pl.ds(0, FACTOR[0])]) for k, ref in enumerate(messages)],
        factor_sems,
    )
    wait_all(saves)


def temporal_input_back_kernel(projected_grad, qkv_w, seed, mod, unit, inverse, result, result_v, sem):
    g = seed[...].reshape(TOK, D).astype(F32)
    normed_grad = dot(projected_grad[...], qkv_w[...]).astype(BF16).astype(F32)
    x_grad = layer_norm_back(normed_grad * (1.0 + mod[0, 1, 1:2, :]), unit[...], inverse[:, 0:1])
    result_v[...] = (g + x_grad).astype(BF16).reshape(FRAMES, 2, D)
    save = pltpu.make_async_copy(result_v, result, sem)
    save.start()
    save.wait()


def block_out_kernel(attended, out_w, located, mod, result, o_v, located_v, result_v, sems):
    copies = fetch([(out_w.at[1], o_v), (located, located_v)], sems.at[pl.ds(0, 2)])
    wait_all(copies)
    x = located_v[...].reshape(TOK, D).astype(F32)
    branch = dot(attended[...], o_v[...])
    result_v[...] = (x + mod[0, 2, 1:2, :] * branch).astype(BF16).reshape(FRAMES, 2, D)
    wait_all(fetch([(result_v, result)], sems.at[pl.ds(2, 1)]))


def weight_grad_kernel(core, *refs):
    messages, branch_grad = refs[0:Y], refs[Y : 2 * Y]
    keep, send_0, send_1, keep_v, send_v, sems = refs[2 * Y :]
    left = lanes_of([m[: FACTOR[0]] for m in messages])
    normed = [lanes_of([m[FACTOR[0] + t * TOK : FACTOR[0] + (t + 1) * TOK] for t in range(D // TOK)]) for m in messages]
    is_qkv = lax.rem(lax.broadcasted_iota(jnp.int32, (PARTS * BLOCK, 1), 0), BLOCK) < QKV_COLS
    from_normed = dot(left, rows_of(normed))
    from_branch = dot(left, rows_of([n[...] for n in branch_grad]))
    sums = jnp.where(is_qkv, from_normed, from_branch)
    tails = sums[:, 1024:].reshape(PARTS, 5, 8, TOK)
    first = core[0] == 0
    copies = []

    def chunk(d):
        main = [sums[:, d * 256 + i * TOK : d * 256 + (i + 1) * TOK].reshape(PARTS, BLOCK, TOK) for i in range(2)]
        packed = jnp.concatenate([tails[:, i, :, d * 32 : (d + 1) * 32] for i in range(4)], axis=-1)
        last = tails[:, 4]
        if d > 0:
            last = jnp.concatenate([last[:, :, d * 32 :], last[:, :, : d * 32]], axis=-1)
        rest = [m[:, 32:36] for m in main]
        whole_chunk = jnp.concatenate([m[:, :32] for m in main] + rest + [packed, last], axis=1)
        return whole_chunk.reshape(FLAT)

    for x in range(2):
        a, b = chunk(2 * x), chunk(2 * x + 1)
        send_v[x] = jnp.where(first, b, a).astype(BF16)
        keep_v[x] = jnp.where(first, a, b).astype(BF16)
        copies += fetch([(send_v.at[x], (send_0, send_1)[x]), (keep_v.at[x], keep.at[x])], sems.at[x])
    wait_all(copies)


def load_kernel(*refs):
    half = len(refs) // 2
    wait_all(fetch(list(zip(refs[:half], refs[half : 2 * half], strict=True)), refs[-1]))


def add_kernel(kept, received_0, received_1, result, result_v, sems):
    copies = []
    for i, received in enumerate((received_0, received_1)):
        result_v[i] = (kept[i].astype(F32) + received[...].astype(F32)).astype(BF16)
        copies += fetch([(result_v.at[i], result.at[i])], sems.at[pl.ds(i, 1)])
    wait_all(copies)


def sum_kernel(parts, qkv, proj, qkv_v, proj_v, sems):
    total = parts[0].astype(F32)
    for i in range(1, 2 * PARTS):
        total = total + parts[i].astype(F32)
    packed, last = total[72:80], total[80:88]
    tail = jnp.concatenate([packed[:, i * 32 : (i + 1) * 32] for i in range(4)] + [last[:4, :32]], axis=0)
    main = [jnp.concatenate([total[:32], total[64:68]], axis=0), jnp.concatenate([total[32:64], total[68:72]], axis=0)]
    full = jnp.concatenate(main + [tail], axis=1)
    qkv_v[...] = full[:QKV_COLS]
    proj_v[...] = full[QKV_COLS : QKV_COLS + PROJ_ROWS]
    wait_all(fetch([(qkv_v, qkv), (proj_v, proj)], sems))


def call(kernel, name, inputs, outputs, scratch=(), mib=24, us=2.0):
    return pl.pallas_call(
        kernel,
        out_shape=tuple(space(shape, dtype) for space, dtype, shape in outputs),
        in_specs=[pl.BlockSpec(memory_space=space) for space, _ in inputs],
        out_specs=tuple(pl.BlockSpec(memory_space=space) for space, _, _ in outputs),
        scratch_shapes=list(scratch),
        compiler_params=pltpu.CompilerParams(vmem_limit_bytes=mib * 2**20),
        cost_estimate=pl.CostEstimate(flops=int(us * 1e9), bytes_accessed=int(us * 3e6), transcendentals=0),
        name=name,
    )(*[pltpu.with_memory_space_constraint(x, space) if space is not pltpu.SMEM else x for space, x in inputs])


def over(axis, size, k, x):
    return lax.ppermute(x, axis, [(i, (i + k) % size) for i in range(size)])


def hbm(n):
    return [pl.BlockSpec(memory_space=pltpu.HBM)] * n


def vmem(n):
    return [pl.BlockSpec(memory_space=pltpu.VMEM)] * n


def whole(*shape):
    return pl.BlockSpec(shape, lambda i: (0,) * len(shape))


def params(mib):
    return pltpu.CompilerParams(vmem_limit_bytes=mib * 2**20)


def out(dtype, *shape):
    return pltpu.HBM(shape, dtype)


def buf(dtype, *shape):
    return pltpu.VMEM(shape, dtype)


def dma(*n):
    return pltpu.SemaphoreType.DMA(n) if n else pltpu.SemaphoreType.DMA


HBM, VMEM, SMEM = pltpu.HBM, pltpu.VMEM, pltpu.SMEM
PAIRS = (FRAMES, 2, D)
MOD = (1, 3, 2, D)
QKV_W = (3 * HW, D)
OUT_W = (HW, D)
ATT = (TOK, HW)
PROB = (HEADS, TOK, TOK)
CHUNK = (88, TOK)
FLAT = (PARTS * 88, TOK)
FACTOR = (PARTS * BLOCK, TOK)
MESSAGE = (FACTOR[0] + D, TOK)


def shards(tokens, modulation, frame_pos, qkv_weight, out_weight, seed_grad):
    seed = seed_grad.reshape(PAIRS)
    tokens = tokens.reshape(TOK, D)
    mod = modulation.transpose(0, 2, 1, 3)
    qkv_w = qkv_weight.swapaxes(1, 2)
    seq = ("y", "xl", "z")

    place = lax.axis_index("y").reshape(1).astype(jnp.int32)
    x1, q, k, v, p = call(
        spatial_forward_kernel,
        "spatial_forward",
        [(SMEM, place), (HBM, tokens), (HBM, mod), (HBM, qkv_w), (HBM, out_weight)],
        [(HBM, BF16, PAIRS), (HBM, BF16, ATT), (HBM, BF16, ATT), (HBM, BF16, ATT), (HBM, BF16, PROB)],
        [
            buf(BF16, TOK, D), buf(F32, *MOD), buf(BF16, *QKV_W), buf(BF16, *OUT_W), buf(BF16, TOK, D),
            buf(BF16, *PAIRS), buf(BF16, *ATT), buf(BF16, *ATT), buf(BF16, *ATT), buf(BF16, *PROB), dma(6), dma(5),
        ],
        us=5.0,
    )
    located = lax.all_to_all(x1, seq, split_axis=0, concat_axis=0, tiled=True)

    later_seed, later_pos, _ = lax.optimization_barrier((seed, frame_pos, x1))
    sent, branch_grad = call(
        branch_grad_kernel,
        "branch_grad",
        [(HBM, later_seed), (VMEM, mod)],
        [(HBM, BF16, (TOK, D)), (HBM, BF16, (TOK, D))],
        [buf(BF16, *PAIRS), buf(BF16, TOK, D), buf(BF16, TOK, D), dma(3)],
        us=2.0,
    )
    branch_all = [sent] + [over("y", Y, i, sent) for i in range(1, Y)]

    cosines, sines = call(
        tables_kernel,
        "tables",
        [(VMEM, later_pos.reshape(1, FRAMES))],
        [(HBM, F32, ATT), (HBM, F32, ATT)],
        [buf(F32, *ATT), buf(F32, *ATT), dma(2)],
        us=1.5,
    )
    located, branch_grad, cosines = lax.optimization_barrier((located, branch_grad, cosines))
    attended, projected_grad, unit, inverse, w1, *messages = call(
        temporal_attention_kernel,
        "temporal_attention",
        [
            (SMEM, place), (VMEM, located), (VMEM, mod), (HBM, cosines), (HBM, sines), (HBM, qkv_w), (HBM, out_weight),
            (HBM, branch_grad),
        ],
        [
            (VMEM, BF16, ATT), (VMEM, BF16, (TOK, 3 * HW)), (VMEM, F32, (TOK, D)), (VMEM, F32, (TOK, TOK)),
            (VMEM, BF16, QKV_W),
        ]
        + [(HBM, BF16, MESSAGE)] * Y,
        [
            buf(BF16, TOK, D), buf(BF16, *OUT_W), buf(F32, *ATT), buf(F32, *ATT), buf(BF16, D, TOK),
            buf(BF16, TOK, D), buf(BF16, 3, *ATT), buf(BF16, Y, *FACTOR), buf(F32, 4 * HW, TOK), dma(7), dma(Y), dma(Y),
        ],
        us=7.0,
    )
    messages = [messages[0]] + [over("y", Y, i, messages[i]) for i in range(1, Y)]
    projected_grad, branch_all = lax.optimization_barrier((projected_grad, branch_all))
    (located_grad,) = call(
        temporal_input_back_kernel,
        "temporal_input_back",
        [(VMEM, projected_grad), (VMEM, w1), (VMEM, seed), (VMEM, mod), (VMEM, unit), (VMEM, inverse)],
        [(HBM, BF16, PAIRS)],
        [buf(BF16, *PAIRS), dma()],
        us=3.0,
    )
    framed_grad = lax.all_to_all(located_grad, seq, split_axis=0, concat_axis=0, tiled=True)

    own_message, own_branch, _ = lax.optimization_barrier((messages[0], branch_all[0], located_grad))
    own_message, own_branch = call(
        load_kernel,
        "load_own",
        [(HBM, own_message), (HBM, own_branch)],
        [(VMEM, BF16, MESSAGE), (VMEM, BF16, (TOK, D))],
        [dma(2)],
        us=1.0,
    )
    messages, branch_all = [own_message] + messages[1:], [own_branch] + branch_all[1:]
    core = lax.axis_index("core").reshape(1).astype(jnp.int32)
    keep, send_0, send_1 = call(
        weight_grad_kernel,
        "weight_grad",
        [(SMEM, core)] + [(VMEM, x) for x in (*messages, *branch_all)],
        [(HBM, BF16, (2, *FLAT)), (HBM, BF16, FLAT), (HBM, BF16, FLAT)],
        [buf(BF16, 2, *FLAT), buf(BF16, 2, *FLAT), dma(2, 2)],
        us=4.6,
    )
    framed_grad, send_1 = lax.optimization_barrier((framed_grad, send_1))
    swap = [(0, 1), (1, 0)]
    received = [lax.ppermute(send, "core", swap) for send in (send_0, send_1)]

    framed_grad, keep_later = lax.optimization_barrier((framed_grad, keep))
    (kept,) = call(
        load_kernel, "load", [(HBM, keep_later)], [(VMEM, BF16, (2, *FLAT))], [dma(1)], us=1.0
    )
    (halves,) = call(
        add_kernel,
        "add_cores",
        [(VMEM, kept), (VMEM, received[0]), (VMEM, received[1])],
        [(HBM, BF16, (2, *FLAT))],
        [buf(BF16, 2, *FLAT), dma(2)],
        us=1.0,
    )
    parts = lax.all_to_all(
        halves.reshape(2 * PARTS, *CHUNK), ("xh", "xl", "z"), split_axis=0, concat_axis=0, tiled=True
    )

    framed_grad, attended, _ = lax.optimization_barrier((framed_grad, attended, halves))
    (projected_grad,) = call(
        spatial_attention_back_kernel,
        "spatial_attention_back",
        [(VMEM, framed_grad), (VMEM, mod), (HBM, out_weight), (HBM, q), (HBM, k), (HBM, v), (HBM, p)],
        [(VMEM, BF16, (TOK, 3 * HW))],
        [buf(BF16, *OUT_W), buf(BF16, *ATT), buf(BF16, *ATT), buf(BF16, *ATT), buf(BF16, *PROB), dma(5)],
        us=3.5,
    )
    (tokens_grad,) = call(
        spatial_input_back_kernel,
        "spatial_input_back",
        [(VMEM, framed_grad), (HBM, tokens), (VMEM, mod), (HBM, qkv_w), (VMEM, projected_grad)],
        [(HBM, BF16, (TOK, D))],
        [buf(BF16, TOK, D), buf(BF16, *QKV_W), buf(BF16, TOK, D), dma(3)],
        us=3.0,
    )
    (block_out,) = call(
        block_out_kernel,
        "block_out",
        [(VMEM, attended), (HBM, out_weight), (HBM, located), (VMEM, mod)],
        [(HBM, BF16, PAIRS)],
        [buf(BF16, *OUT_W), buf(BF16, *PAIRS), buf(BF16, *PAIRS), dma(3)],
        us=2.0,
    )
    qkv_grad, proj_grad = call(
        sum_kernel,
        "sum_parts",
        [(VMEM, parts)],
        [(HBM, F32, (QKV_COLS, WIDTH)), (HBM, F32, (PROJ_ROWS, WIDTH))],
        [buf(F32, QKV_COLS, WIDTH), buf(F32, PROJ_ROWS, WIDTH), dma(2)],
        us=1.5,
    )
    return (
        block_out.reshape(1, FRAMES, 2, D),
        tokens_grad.reshape(1, 1, LOC, D),
        qkv_grad.T,
        proj_grad,
    )


def solution(mesh):
    sizes = (2, 2, 4, 2, 8)
    split = Mesh(mesh.devices.reshape(sizes), ("xh", "core", "y", "xl", "z"))
    dp, seq = ("xh", "core"), ("y", "xl", "z")
    return jax.shard_map(
        shards,
        mesh=split,
        in_specs=(
            P(dp, seq, None, None),
            P(dp, None, None, None),
            P(),
            P(),
            P(),
            P(dp, None, seq, None),
        ),
        out_specs=(
            P(dp, None, seq, None),
            P(dp, seq, None, None),
            P(dp, seq),
            P(seq, dp),
        ),
        check_vma=False,
    )
```

```python
from functools import partial
import math

import jax
import jax.numpy as jnp
import numpy as np
from jax import lax
from jax.experimental import pallas as pl
from jax.experimental.pallas import tpu as pltpu
from jax.sharding import Mesh, PartitionSpec as P

D = 1152
HEADS = 8
HEAD_DIM = 72
HALF = HEAD_DIM // 2
HW = 576
LOC = 128
FRAMES = 64
TOK = 128
SCALE = HEAD_DIM ** (-0.5)
EPS = 1e-06
ROPE_BASE = 10000.0
QKV_COLS = 27
PROJ_ROWS = 9
BLOCK = 40
Y = 4
PARTS = 16
WIDTH = D // 4
F32 = jnp.float32
BF16 = jnp.bfloat16

NN = (((1,), (0,)), ((), ()))
NT = (((1,), (1,)), ((), ()))
TN = (((0,), (0,)), ((), ()))


def dot(a, b, dims=NN):
    return lax.dot_general(a, b, dims, preferred_element_type=F32)


def layer_norm(x):
    centered = x - jnp.mean(x, axis=-1, keepdims=True)
    inverse = lax.rsqrt(jnp.mean(centered * centered, axis=-1, keepdims=True) + EPS)
    return centered * inverse, inverse


def layer_norm_back(grad, unit, inverse):
    first = jnp.mean(grad, axis=-1, keepdims=True)
    second = jnp.mean(grad * unit, axis=-1, keepdims=True)
    return inverse * (grad - first - unit * second)


def split_heads(x):
    lane = lax.broadcasted_iota(jnp.int32, (1, HW), 1)
    parts = []
    for h in range(HEADS):
        mine = ((lane >= h * HEAD_DIM) & (lane < (h + 1) * HEAD_DIM)).astype(F32).astype(BF16)
        parts.append(x * mine)
    return jnp.concatenate(parts, axis=0)


def head(x, h):
    return x[:, h * TOK : (h + 1) * TOK]


def rows_of(parts):
    return jnp.concatenate(parts, axis=0)


def lanes_of(parts):
    return jnp.concatenate(parts, axis=1)


def attend(query, keys_by_head, values_by_head, allowed):
    scores = dot(query, keys_by_head, NT)
    probs = []
    for h in range(HEADS):
        s = head(scores, h) * SCALE
        if allowed is not None:
            s = jnp.where(allowed, s, -1e30)
        e = jnp.exp(s - jnp.max(s, axis=-1, keepdims=True))
        probs.append((e / jnp.sum(e, axis=-1, keepdims=True)).astype(BF16))
    return probs, dot(lanes_of(probs), values_by_head).astype(BF16)


def attend_back(probs, attended_grad, query, keys_by_head, values_by_head):
    prob_grads = dot(attended_grad, values_by_head, NT)
    values_grad = dot(rows_of(probs), split_heads(attended_grad), TN)
    score_grads = []
    for h in range(HEADS):
        p = probs[h].astype(F32)
        g = head(prob_grads, h)
        s = p * (g - jnp.sum(g * p, axis=-1, keepdims=True)) * SCALE
        score_grads.append(s.astype(BF16))
    query_grad = dot(lanes_of(score_grads), keys_by_head)
    keys_grad = dot(rows_of(score_grads), split_heads(query), TN)
    return query_grad, keys_grad, values_grad


def swap_halves(x):
    lane = lax.broadcasted_iota(jnp.int32, (1, HW), 1)
    first = lax.rem(lane, HEAD_DIM) < HALF
    later = jnp.concatenate([x[:, HALF:], x[:, :HALF]], axis=1)
    earlier = jnp.concatenate([x[:, HW - HALF :], x[:, : HW - HALF]], axis=1)
    return jnp.where(first, later, earlier)


def fetch(pairs, sems):
    copies = [pltpu.make_async_copy(src, dst, sems.at[i]) for i, (src, dst) in enumerate(pairs)]
    for c in copies:
        c.start()
    return copies


def store(pairs, sems):
    return fetch(pairs, sems)


def start_all(copies):
    for c in copies:
        c.start()


def wait_all(copies):
    for c in copies:
        c.wait()


def regroup(x):
    main = [x[:, d * WIDTH : d * WIDTH + 256] for d in range(4)]
    tail = [x[:, d * WIDTH + 256 : (d + 1) * WIDTH] for d in range(4)]
    return jnp.concatenate(main + tail, axis=1)


def rope_tables(pos):
    row = lax.broadcasted_iota(jnp.int32, (TOK, FRAMES), 0)
    frame = lax.broadcasted_iota(jnp.int32, (TOK, FRAMES), 1)
    mine = (row >= 2 * frame) & (row < 2 * frame + 2)
    time = jnp.sum(jnp.where(mine, pos.astype(F32), 0.0), axis=-1, keepdims=True)
    lane = lax.broadcasted_iota(jnp.int32, (1, HW), 1)
    frequency = jnp.exp(lax.rem(lane, HALF).astype(F32) * (-2.0 * math.log(ROPE_BASE) / HEAD_DIM))
    angles = time * frequency
    sign = jnp.where(lax.rem(lane, HEAD_DIM) < HALF, -1.0, 1.0)
    return jnp.cos(angles), jnp.sin(angles) * sign


def branch_grad_kernel(
    seed, pos, mod, sent, kept, cos_out, sin_out, seed_v, sent_v, kept_v, cos_v, sin_v, sems
):
    (load,) = fetch([(seed, seed_v)], sems.at[pl.ds(0, 1)])
    cos_v[...], sin_v[...] = rope_tables(pos[...])
    saves = fetch([(cos_v, cos_out), (sin_v, sin_out)], sems.at[pl.ds(1, 2)])
    load.wait()
    g = seed_v[...].reshape(TOK, D).astype(F32)
    branch_grad = (mod[0, 2, 1:2, :] * g).astype(BF16)
    sent_v[...] = regroup(branch_grad)
    kept_v[...] = branch_grad
    wait_all(saves + fetch([(sent_v, sent), (kept_v, kept)], sems.at[pl.ds(3, 2)]))


def spatial_forward_kernel(
    place, tokens, mod, qkv_w, out_w, x1, q_out, k_out, v_out, p_out,
    tokens_v, mod_v, w_v, o_v, normed_v, x1_v, q_v, k_v, v_v, p_v, in_sem, out_sem,
):
    pairs = [(tokens, tokens_v), (mod, mod_v)]
    pairs += [(qkv_w.at[0, pl.ds(i * HW, HW)], w_v.at[pl.ds(i * HW, HW)]) for i in range(3)] + [(out_w.at[0], o_v)]
    copies = [pltpu.make_async_copy(src, dst, in_sem.at[i]) for i, (src, dst) in enumerate(pairs)]
    start_all(copies)
    wait_all(copies[:2])

    @pl.when(place[0] >= 0)
    def _():
        unit, _ = layer_norm(tokens_v[...].astype(F32))
        normed_v[...] = (unit * (1.0 + mod_v[0, 1, 0:1, :]) + mod_v[0, 0, 0:1, :]).astype(BF16)

    for i, held in enumerate((q_v, k_v, v_v)):
        copies[2 + i].wait()

        @pl.when(place[0] >= 0)
        def _(i=i, held=held):
            held[...] = dot(normed_v[...], w_v[i * HW : (i + 1) * HW, :], NT).astype(BF16)

    probs, attended = attend(q_v[...], split_heads(k_v[...]), split_heads(v_v[...]), None)
    for h in range(HEADS):
        p_v[h] = probs[h]
    saves = fetch([(q_v, q_out), (k_v, k_out), (v_v, v_out), (p_v, p_out)], out_sem.at[pl.ds(0, 4)])
    copies[5].wait()
    branch = dot(attended, o_v[...])
    x1_v[...] = (tokens_v[...].astype(F32) + mod_v[0, 2, 0:1, :] * branch).astype(BF16).reshape(FRAMES, 2, D)
    saves += fetch([(x1_v, x1)], out_sem.at[pl.ds(4, 1)])
    wait_all(saves)


def spatial_attention_back_kernel(
    grad, mod, out_w, q_in, k_in, v_in, p_in, result, o_v, q_v, k_v, v_v, p_v, sems
):
    copies = fetch([(out_w.at[0], o_v), (v_in, v_v), (p_in, p_v), (k_in, k_v), (q_in, q_v)], sems)
    g = grad[...].reshape(TOK, D).astype(F32)
    branch_grad = (mod[0, 2, 0:1, :] * g).astype(BF16)
    wait_all(copies)
    attended_grad = dot(branch_grad, o_v[...], NT).astype(BF16)
    probs = [p_v[h] for h in range(HEADS)]
    grads = attend_back(probs, attended_grad, q_v[...], split_heads(k_v[...]), split_heads(v_v[...]))
    result[...] = lanes_of(grads).astype(BF16)


def spatial_input_back_kernel(grad, tokens, mod, qkv_w, projected_grad, result, tokens_v, w_v, result_v, sems):
    copies = fetch([(tokens, tokens_v), (qkv_w.at[0], w_v)], sems.at[pl.ds(0, 2)])
    copies[0].wait()
    g = grad[...].reshape(TOK, D).astype(F32)
    unit, inverse = layer_norm(tokens_v[...].astype(F32))
    copies[1].wait()
    normed_grad = dot(projected_grad[...], w_v[...]).astype(BF16).astype(F32)
    x_grad = layer_norm_back(normed_grad * (1.0 + mod[0, 1, 0:1, :]), unit, inverse)
    result_v[...] = (g + x_grad).astype(BF16)
    wait_all(fetch([(result_v, result)], sems.at[pl.ds(2, 1)]))


def temporal_normed_kernel(located, mod, sent, grouped_out, kept, unit_out, inverse_out, sem):
    unit, inverse = layer_norm(located[...].reshape(TOK, D).astype(F32))
    normed = (unit * (1.0 + mod[0, 1, 1:2, :]) + mod[0, 0, 1:2, :]).astype(BF16)
    grouped = regroup(normed)
    grouped_out[...] = rows_of([grouped[:, t * TOK : (t + 1) * TOK] for t in range(D // TOK)])
    save = pltpu.make_async_copy(grouped_out, sent, sem)
    save.start()
    kept[...] = normed
    unit_out[...] = unit
    inverse_out[...] = jnp.broadcast_to(inverse, (TOK, TOK))
    save.wait()


def temporal_attention_kernel(
    place, normed, grouped, cosines, sines, qkv_w, out_w, branch_grad,
    attended_out, normed_grad, own, to_1, to_2, to_3,
    w_out, branch_v, o_v, cos_v, sin_v, qkv_v, factors_v, wide, in_sems, sems, factor_sems,
):
    pairs = [(qkv_w.at[1, pl.ds(i * HW, HW)], w_out.at[pl.ds(i * HW, HW)]) for i in range(3)]
    pairs += [(cosines, cos_v), (sines, sin_v), (out_w.at[1], o_v), (branch_grad, branch_v)]
    copies = fetch(pairs, in_sems)
    messages = (own, to_1, to_2, to_3)
    saves = fetch([(grouped, ref.at[pl.ds(FACTOR[0], D)]) for ref in (own, to_1, to_3)], sems)
    for i in range(3):
        copies[i].wait()

        @pl.when(place[0] >= 0)
        def _(i=i):
            qkv_v[i] = dot(normed[...], w_out[i * HW : (i + 1) * HW, :], NT).astype(BF16)

    parts = [qkv_v[i] for i in range(3)]
    wait_all(copies[3:5])
    cos, sin = cos_v[...], sin_v[...]

    def rotate(t):
        t = t.astype(F32)
        return (t * cos + swap_halves(t) * sin).astype(BF16)

    def rotate_back(t):
        t = t.astype(BF16).astype(F32)
        return t * cos + swap_halves(t * sin)

    q, k, v = rotate(parts[0]), rotate(parts[1]), parts[2]
    keys_by_head, values_by_head = split_heads(k), split_heads(v)
    row = lax.broadcasted_iota(jnp.int32, (TOK, TOK), 0)
    column = lax.broadcasted_iota(jnp.int32, (TOK, TOK), 1)
    same = lax.rem(row, 2) == lax.rem(column, 2)
    probs, attended = attend(q, keys_by_head, values_by_head, same)
    attended_out[...] = attended
    wait_all(copies[5:])
    attended_grad = dot(branch_v[...], o_v[...], NT).astype(BF16)
    q_grad, k_grad, v_grad = attend_back(probs, attended_grad, q, keys_by_head, values_by_head)
    grads = lanes_of([rotate_back(q_grad), rotate_back(k_grad), v_grad])

    wide[: 3 * HW, :] = grads.T
    wide[3 * HW :, :] = attended.astype(F32).T
    empty = jnp.zeros((BLOCK - QKV_COLS - PROJ_ROWS, TOK), F32)
    for y in range(Y):
        pieces = []
        for s in range(PARTS):
            i = y * PARTS + s
            pieces += [
                wide[pl.ds(i * QKV_COLS, QKV_COLS), :],
                wide[pl.ds(3 * HW + i * PROJ_ROWS, PROJ_ROWS), :],
                empty,
            ]
        factors_v[y] = jnp.concatenate(pieces, axis=0).astype(BF16)
    saves += fetch(
        [(factors_v.at[lax.rem(place[0] + k, Y)], ref.at[pl.ds(0, FACTOR[0])]) for k, ref in enumerate(messages)],
        factor_sems,
    )
    normed_grad[...] = dot(grads.astype(BF16), w_out[...]).astype(BF16)
    wait_all(saves)


def temporal_input_back_kernel(normed_grad, seed, mod, unit, inverse, result, result_v, sem):
    g = seed[...].reshape(TOK, D).astype(F32)
    x_grad = layer_norm_back(normed_grad[...].astype(F32) * (1.0 + mod[0, 1, 1:2, :]), unit[...], inverse[:, 0:1])
    result_v[...] = (g + x_grad).astype(BF16).reshape(FRAMES, 2, D)
    save = pltpu.make_async_copy(result_v, result, sem)
    save.start()
    save.wait()


def block_out_kernel(attended, out_w, located, mod, result, o_v, located_v, result_v, sems):
    copies = fetch([(out_w.at[1], o_v), (located, located_v)], sems.at[pl.ds(0, 2)])
    wait_all(copies)
    x = located_v[...].reshape(TOK, D).astype(F32)
    branch = dot(attended[...], o_v[...])
    result_v[...] = (x + mod[0, 2, 1:2, :] * branch).astype(BF16).reshape(FRAMES, 2, D)
    wait_all(fetch([(result_v, result)], sems.at[pl.ds(2, 1)]))


def weight_grad_kernel(core, *refs):
    messages, branch_grad, normed_far = refs[0:Y], refs[Y : 2 * Y], refs[2 * Y]
    keep, *sends = refs[2 * Y + 1 : 2 * Y + 2 + PIECES]
    keep_v, send_v, sems = refs[2 * Y + 2 + PIECES :]
    left = lanes_of([m[: FACTOR[0]] for m in messages])
    normed = []
    for k, m in enumerate(messages):
        ref, at = (normed_far, 0) if k == 2 else (m, FACTOR[0])
        normed.append(lanes_of([ref[at + t * TOK : at + (t + 1) * TOK] for t in range(D // TOK)]))
    is_qkv = lax.rem(lax.broadcasted_iota(jnp.int32, (PARTS * BLOCK, 1), 0), BLOCK) < QKV_COLS
    from_normed = dot(left, rows_of(normed))
    from_branch = dot(left, rows_of([n[...] for n in branch_grad]))
    sums = jnp.where(is_qkv, from_normed, from_branch)
    tails = sums[:, 1024:].reshape(PARTS, 5, 8, TOK)
    first = core[0] == 0
    copies = []

    def chunk(d):
        main = [sums[:, d * 256 + i * TOK : d * 256 + (i + 1) * TOK].reshape(PARTS, BLOCK, TOK) for i in range(2)]
        packed = jnp.concatenate([tails[:, i, :, d * 32 : (d + 1) * 32] for i in range(4)], axis=-1)
        last = tails[:, 4]
        if d > 0:
            last = jnp.concatenate([last[:, :, d * 32 :], last[:, :, : d * 32]], axis=-1)
        rest = [m[:, 32:36] for m in main]
        whole_chunk = jnp.concatenate([m[:, :32] for m in main] + rest + [packed, last], axis=1)
        return whole_chunk.reshape(FLAT)

    for x in range(2):
        a, b = chunk(2 * x), chunk(2 * x + 1)
        send_v[x] = jnp.where(first, b, a).astype(BF16)
        keep_v[x] = jnp.where(first, a, b).astype(BF16)
        each = PIECES // 2
        pairs = [(send_v.at[x, pl.ds(i * PIECE[0], PIECE[0])], sends[x * each + i]) for i in range(each)]
        copies += fetch(pairs + [(keep_v.at[x], keep.at[x])], sems.at[x])
    wait_all(copies)


def load_kernel(*refs):
    half = len(refs) // 2
    wait_all(fetch(list(zip(refs[:half], refs[half : 2 * half], strict=True)), refs[-1]))


def add_kernel(kept, *refs):
    received, (result, result_v, sems) = refs[:PIECES], refs[PIECES:]
    copies = []
    for i, piece in enumerate(received):
        half, rows = i // (PIECES // 2), pl.ds(i % (PIECES // 2) * PIECE[0], PIECE[0])
        result_v[half, rows] = (kept[half, rows].astype(F32) + piece[...].astype(F32)).astype(BF16)
        if i % (PIECES // 2) == PIECES // 2 - 1:
            copies += fetch([(result_v.at[half], result.at[half])], sems.at[pl.ds(half, 1)])
    wait_all(copies)


def sum_kernel(parts, qkv, proj, qkv_v, proj_v, sems):
    total = parts[0].astype(F32)
    for i in range(1, 2 * PARTS):
        total = total + parts[i].astype(F32)
    packed, last = total[72:80], total[80:88]
    tail = jnp.concatenate([packed[:, i * 32 : (i + 1) * 32] for i in range(4)] + [last[:4, :32]], axis=0)
    main = [jnp.concatenate([total[:32], total[64:68]], axis=0), jnp.concatenate([total[32:64], total[68:72]], axis=0)]
    full = jnp.concatenate(main + [tail], axis=1)
    qkv_v[...] = full[:QKV_COLS]
    proj_v[...] = full[QKV_COLS : QKV_COLS + PROJ_ROWS]
    wait_all(fetch([(qkv_v, qkv), (proj_v, proj)], sems))


def call(kernel, name, inputs, outputs, scratch=(), mib=24, us=2.0):
    return pl.pallas_call(
        kernel,
        out_shape=tuple(space(shape, dtype) for space, dtype, shape in outputs),
        in_specs=[pl.BlockSpec(memory_space=space) for space, _ in inputs],
        out_specs=tuple(pl.BlockSpec(memory_space=space) for space, _, _ in outputs),
        scratch_shapes=list(scratch),
        compiler_params=pltpu.CompilerParams(vmem_limit_bytes=mib * 2**20),
        cost_estimate=pl.CostEstimate(flops=int(us * 1e9), bytes_accessed=int(us * 3e6), transcendentals=0),
        name=name,
    )(*[pltpu.with_memory_space_constraint(x, space) if space is not pltpu.SMEM else x for space, x in inputs])


def over(axis, size, k, x):
    return lax.ppermute(x, axis, [(i, (i + k) % size) for i in range(size)])


def hbm(n):
    return [pl.BlockSpec(memory_space=pltpu.HBM)] * n


def vmem(n):
    return [pl.BlockSpec(memory_space=pltpu.VMEM)] * n


def whole(*shape):
    return pl.BlockSpec(shape, lambda i: (0,) * len(shape))


def params(mib):
    return pltpu.CompilerParams(vmem_limit_bytes=mib * 2**20)


def out(dtype, *shape):
    return pltpu.HBM(shape, dtype)


def buf(dtype, *shape):
    return pltpu.VMEM(shape, dtype)


def dma(*n):
    return pltpu.SemaphoreType.DMA(n) if n else pltpu.SemaphoreType.DMA


HBM, VMEM, SMEM = pltpu.HBM, pltpu.VMEM, pltpu.SMEM
PAIRS = (FRAMES, 2, D)
MOD = (1, 3, 2, D)
QKV_W = (3 * HW, D)
OUT_W = (HW, D)
ATT = (TOK, HW)
PROB = (HEADS, TOK, TOK)
CHUNK = (88, TOK)
FLAT = (PARTS * 88, TOK)
PIECES = 2
PIECE = (2 * FLAT[0] // PIECES, TOK)
FACTOR = (PARTS * BLOCK, TOK)
MESSAGE = (FACTOR[0] + D, TOK)


def shards(tokens, modulation, frame_pos, qkv_weight, out_weight, seed_grad):
    seed = seed_grad.reshape(PAIRS)
    tokens = tokens.reshape(TOK, D)
    mod = modulation.transpose(0, 2, 1, 3)
    qkv_w = qkv_weight.swapaxes(1, 2)
    seq = ("y", "xl", "z")

    place = lax.axis_index("y").reshape(1).astype(jnp.int32)
    x1, q, k, v, p = call(
        spatial_forward_kernel,
        "spatial_forward",
        [(SMEM, place), (HBM, tokens), (HBM, mod), (HBM, qkv_w), (HBM, out_weight)],
        [(HBM, BF16, PAIRS), (HBM, BF16, ATT), (HBM, BF16, ATT), (HBM, BF16, ATT), (HBM, BF16, PROB)],
        [
            buf(BF16, TOK, D), buf(F32, *MOD), buf(BF16, *QKV_W), buf(BF16, *OUT_W), buf(BF16, TOK, D),
            buf(BF16, *PAIRS), buf(BF16, *ATT), buf(BF16, *ATT), buf(BF16, *ATT), buf(BF16, *PROB), dma(6), dma(5),
        ],
        us=5.0,
    )
    located = lax.all_to_all(x1, seq, split_axis=0, concat_axis=0, tiled=True)

    later_seed, later_pos, _ = lax.optimization_barrier((seed, frame_pos, x1))
    sent, branch_grad, cosines, sines = call(
        branch_grad_kernel,
        "branch_grad",
        [(HBM, later_seed), (VMEM, later_pos.reshape(1, FRAMES)), (VMEM, mod)],
        [(HBM, BF16, (TOK, D)), (HBM, BF16, (TOK, D)), (HBM, F32, ATT), (HBM, F32, ATT)],
        [buf(BF16, *PAIRS), buf(BF16, TOK, D), buf(BF16, TOK, D), buf(F32, *ATT), buf(F32, *ATT), dma(5)],
        us=3.0,
    )
    branch_all = [sent] + [over("y", Y, i, sent) for i in range(1, Y)]

    located, branch_grad, cosines = lax.optimization_barrier((located, branch_grad, cosines))
    normed, grouped, normed_here, unit, inverse = call(
        temporal_normed_kernel,
        "temporal_normed",
        [(VMEM, located), (VMEM, mod)],
        [
            (HBM, BF16, (D, TOK)), (VMEM, BF16, (D, TOK)), (VMEM, BF16, (TOK, D)), (VMEM, F32, (TOK, D)),
            (VMEM, F32, (TOK, TOK)),
        ],
        [dma()],
        us=1.5,
    )
    normed_far = over("y", Y, 2, normed)

    attended, normed_grad, *messages = call(
        temporal_attention_kernel,
        "temporal_attention",
        [
            (SMEM, place), (VMEM, normed_here), (VMEM, grouped), (HBM, cosines), (HBM, sines), (HBM, qkv_w),
            (HBM, out_weight), (HBM, branch_grad),
        ],
        [(VMEM, BF16, ATT), (VMEM, BF16, (TOK, D))]
        + [(HBM, BF16, shape) for shape in (MESSAGE, MESSAGE, FACTOR, MESSAGE)],
        [
            buf(BF16, *QKV_W), buf(BF16, TOK, D), buf(BF16, *OUT_W), buf(F32, *ATT), buf(F32, *ATT), buf(BF16, 3, *ATT),
            buf(BF16, Y, *FACTOR), buf(F32, 4 * HW, TOK), dma(7), dma(3), dma(Y),
        ],
        us=7.0,
    )
    messages = [messages[0]] + [over("y", Y, i, messages[i]) for i in range(1, Y)]
    normed_grad, branch_all, normed_far = lax.optimization_barrier((normed_grad, branch_all, normed_far))
    (located_grad,) = call(
        temporal_input_back_kernel,
        "temporal_input_back",
        [(VMEM, normed_grad), (VMEM, seed), (VMEM, mod), (VMEM, unit), (VMEM, inverse)],
        [(HBM, BF16, PAIRS)],
        [buf(BF16, *PAIRS), dma()],
        us=3.0,
    )
    framed_grad = lax.all_to_all(located_grad, seq, split_axis=0, concat_axis=0, tiled=True)

    own_message, own_branch, _ = lax.optimization_barrier((messages[0], branch_all[0], located_grad))
    own_message, own_branch = call(
        load_kernel,
        "load_own",
        [(HBM, own_message), (HBM, own_branch)],
        [(VMEM, BF16, MESSAGE), (VMEM, BF16, (TOK, D))],
        [dma(2)],
        us=1.0,
    )
    messages, branch_all = [own_message] + messages[1:], [own_branch] + branch_all[1:]
    core = lax.axis_index("core").reshape(1).astype(jnp.int32)
    keep, *sends = call(
        weight_grad_kernel,
        "weight_grad",
        [(SMEM, core)] + [(VMEM, x) for x in (*messages, *branch_all, normed_far)],
        [(HBM, BF16, (2, *FLAT))] + [(HBM, BF16, PIECE)] * PIECES,
        [buf(BF16, 2, *FLAT), buf(BF16, 2, *FLAT), dma(2, 1 + PIECES // 2)],
        us=4.6,
    )
    swap = [(0, 1), (1, 0)]
    received = [lax.ppermute(send, "core", swap) for send in sends]

    (kept,) = call(
        load_kernel, "load", [(HBM, keep)], [(VMEM, BF16, (2, *FLAT))], [dma(1)], us=1.0
    )
    (halves,) = call(
        add_kernel,
        "add_cores",
        [(VMEM, kept)] + [(VMEM, x) for x in received],
        [(HBM, BF16, (2, *FLAT))],
        [buf(BF16, 2, *FLAT), dma(2)],
        us=1.0,
    )
    framed_grad, halves = lax.optimization_barrier((framed_grad, halves))
    parts = lax.all_to_all(
        halves.reshape(2 * PARTS, *CHUNK), ("xh", "xl", "z"), split_axis=0, concat_axis=0, tiled=True
    )

    framed_grad, attended, _ = lax.optimization_barrier((framed_grad, attended, halves))
    (projected_grad,) = call(
        spatial_attention_back_kernel,
        "spatial_attention_back",
        [(VMEM, framed_grad), (VMEM, mod), (HBM, out_weight), (HBM, q), (HBM, k), (HBM, v), (HBM, p)],
        [(VMEM, BF16, (TOK, 3 * HW))],
        [buf(BF16, *OUT_W), buf(BF16, *ATT), buf(BF16, *ATT), buf(BF16, *ATT), buf(BF16, *PROB), dma(5)],
        us=3.5,
    )
    (tokens_grad,) = call(
        spatial_input_back_kernel,
        "spatial_input_back",
        [(VMEM, framed_grad), (HBM, tokens), (VMEM, mod), (HBM, qkv_w), (VMEM, projected_grad)],
        [(HBM, BF16, (TOK, D))],
        [buf(BF16, TOK, D), buf(BF16, *QKV_W), buf(BF16, TOK, D), dma(3)],
        us=3.0,
    )
    (block_out,) = call(
        block_out_kernel,
        "block_out",
        [(VMEM, attended), (HBM, out_weight), (HBM, located), (VMEM, mod)],
        [(HBM, BF16, PAIRS)],
        [buf(BF16, *OUT_W), buf(BF16, *PAIRS), buf(BF16, *PAIRS), dma(3)],
        us=2.0,
    )
    qkv_grad, proj_grad = call(
        sum_kernel,
        "sum_parts",
        [(VMEM, parts)],
        [(HBM, F32, (QKV_COLS, WIDTH)), (HBM, F32, (PROJ_ROWS, WIDTH))],
        [buf(F32, QKV_COLS, WIDTH), buf(F32, PROJ_ROWS, WIDTH), dma(2)],
        us=1.5,
    )
    return (
        block_out.reshape(1, FRAMES, 2, D),
        tokens_grad.reshape(1, 1, LOC, D),
        qkv_grad.T,
        proj_grad,
    )


def solution(mesh):
    sizes = (2, 2, 4, 2, 8)
    split = Mesh(mesh.devices.reshape(sizes), ("xh", "core", "y", "xl", "z"))
    dp, seq = ("xh", "core"), ("y", "xl", "z")
    return jax.shard_map(
        shards,
        mesh=split,
        in_specs=(
            P(dp, seq, None, None),
            P(dp, None, None, None),
            P(),
            P(),
            P(),
            P(dp, None, seq, None),
        ),
        out_specs=(
            P(dp, None, seq, None),
            P(dp, seq, None, None),
            P(dp, seq),
            P(seq, dp),
        ),
        check_vma=False,
    )
```

```python
from functools import partial
import math

import jax
import jax.numpy as jnp
import numpy as np
from jax import lax
from jax.experimental import pallas as pl
from jax.experimental.pallas import tpu as pltpu
from jax.sharding import Mesh, PartitionSpec as P

D = 1152
HEADS = 8
HEAD_DIM = 72
HALF = HEAD_DIM // 2
HW = 576
LOC = 128
FRAMES = 64
TOK = 128
SCALE = HEAD_DIM ** (-0.5)
EPS = 1e-06
ROPE_BASE = 10000.0
QKV_COLS = 27
PROJ_ROWS = 9
BLOCK = 40
Y = 4
PARTS = 16
WIDTH = D // 4
F32 = jnp.float32
BF16 = jnp.bfloat16

NN = (((1,), (0,)), ((), ()))
NT = (((1,), (1,)), ((), ()))
TN = (((0,), (0,)), ((), ()))


def dot(a, b, dims=NN):
    return lax.dot_general(a, b, dims, preferred_element_type=F32)


def layer_norm(x):
    centered = x - jnp.mean(x, axis=-1, keepdims=True)
    inverse = lax.rsqrt(jnp.mean(centered * centered, axis=-1, keepdims=True) + EPS)
    return centered * inverse, inverse


def layer_norm_back(grad, unit, inverse):
    first = jnp.mean(grad, axis=-1, keepdims=True)
    second = jnp.mean(grad * unit, axis=-1, keepdims=True)
    return inverse * (grad - first - unit * second)


def split_heads(x):
    lane = lax.broadcasted_iota(jnp.int32, (1, HW), 1)
    parts = []
    for h in range(HEADS):
        mine = ((lane >= h * HEAD_DIM) & (lane < (h + 1) * HEAD_DIM)).astype(F32).astype(BF16)
        parts.append(x * mine)
    return jnp.concatenate(parts, axis=0)


def head(x, h):
    return x[:, h * TOK : (h + 1) * TOK]


def rows_of(parts):
    return jnp.concatenate(parts, axis=0)


def lanes_of(parts):
    return jnp.concatenate(parts, axis=1)


def attend(query, keys_by_head, values_by_head, allowed):
    scores = dot(query, keys_by_head, NT)
    probs = []
    for h in range(HEADS):
        s = head(scores, h) * SCALE
        if allowed is not None:
            s = jnp.where(allowed, s, -1e30)
        e = jnp.exp(s - jnp.max(s, axis=-1, keepdims=True))
        probs.append((e / jnp.sum(e, axis=-1, keepdims=True)).astype(BF16))
    return probs, dot(lanes_of(probs), values_by_head).astype(BF16)


def attend_back(probs, attended_grad, query, keys_by_head, values_by_head):
    prob_grads = dot(attended_grad, values_by_head, NT)
    values_grad = dot(rows_of(probs), split_heads(attended_grad), TN)
    score_grads = []
    for h in range(HEADS):
        p = probs[h].astype(F32)
        g = head(prob_grads, h)
        s = p * (g - jnp.sum(g * p, axis=-1, keepdims=True)) * SCALE
        score_grads.append(s.astype(BF16))
    query_grad = dot(lanes_of(score_grads), keys_by_head)
    keys_grad = dot(rows_of(score_grads), split_heads(query), TN)
    return query_grad, keys_grad, values_grad


def swap_halves(x):
    lane = lax.broadcasted_iota(jnp.int32, (1, HW), 1)
    first = lax.rem(lane, HEAD_DIM) < HALF
    later = jnp.concatenate([x[:, HALF:], x[:, :HALF]], axis=1)
    earlier = jnp.concatenate([x[:, HW - HALF :], x[:, : HW - HALF]], axis=1)
    return jnp.where(first, later, earlier)


def fetch(pairs, sems):
    copies = [pltpu.make_async_copy(src, dst, sems.at[i]) for i, (src, dst) in enumerate(pairs)]
    for c in copies:
        c.start()
    return copies


def store(pairs, sems):
    return fetch(pairs, sems)


def start_all(copies):
    for c in copies:
        c.start()


def wait_all(copies):
    for c in copies:
        c.wait()


def regroup(x):
    main = [x[:, d * WIDTH : d * WIDTH + 256] for d in range(4)]
    tail = [x[:, d * WIDTH + 256 : (d + 1) * WIDTH] for d in range(4)]
    return jnp.concatenate(main + tail, axis=1)


def rope_tables(pos):
    row = lax.broadcasted_iota(jnp.int32, (TOK, FRAMES), 0)
    frame = lax.broadcasted_iota(jnp.int32, (TOK, FRAMES), 1)
    mine = (row >= 2 * frame) & (row < 2 * frame + 2)
    time = jnp.sum(jnp.where(mine, pos.astype(F32), 0.0), axis=-1, keepdims=True)
    lane = lax.broadcasted_iota(jnp.int32, (1, HW), 1)
    frequency = jnp.exp(lax.rem(lane, HALF).astype(F32) * (-2.0 * math.log(ROPE_BASE) / HEAD_DIM))
    angles = time * frequency
    sign = jnp.where(lax.rem(lane, HEAD_DIM) < HALF, -1.0, 1.0)
    return jnp.cos(angles), jnp.sin(angles) * sign


def tables_kernel(pos, cos_out, sin_out, cos_v, sin_v, sems):
    cos_v[...], sin_v[...] = rope_tables(pos[...])
    wait_all(fetch([(cos_v, cos_out), (sin_v, sin_out)], sems))


def spatial_forward_kernel(
    place, tokens, mod, qkv_w, out_w, seed, x1, q_out, k_out, v_out, p_out, sent, kept,
    seed_v, sent_v, kept_v, tokens_v, mod_v, w_v, o_v, normed_v, x1_v, q_v, k_v, v_v, p_v, in_sem, out_sem,
):
    pairs = [(tokens, tokens_v), (mod, mod_v), (seed, seed_v)]
    pairs += [(qkv_w.at[0, pl.ds(i * HW, HW)], w_v.at[pl.ds(i * HW, HW)]) for i in range(3)] + [(out_w.at[0], o_v)]
    copies = [pltpu.make_async_copy(src, dst, in_sem.at[i]) for i, (src, dst) in enumerate(pairs)]
    start_all(copies)
    wait_all(copies[:3])

    @pl.when(place[0] >= 0)
    def _():
        unit, _ = layer_norm(tokens_v[...].astype(F32))
        normed_v[...] = (unit * (1.0 + mod_v[0, 1, 0:1, :]) + mod_v[0, 0, 0:1, :]).astype(BF16)
        branch_grad = (mod_v[0, 2, 1:2, :] * seed_v[...].reshape(TOK, D).astype(F32)).astype(BF16)
        sent_v[...] = regroup(branch_grad)
        kept_v[...] = branch_grad

    saves = fetch([(sent_v, sent), (kept_v, kept)], out_sem.at[pl.ds(5, 2)])

    for i, held in enumerate((q_v, k_v, v_v)):
        copies[3 + i].wait()

        @pl.when(place[0] >= 0)
        def _(i=i, held=held):
            held[...] = dot(normed_v[...], w_v[i * HW : (i + 1) * HW, :], NT).astype(BF16)

    probs, attended = attend(q_v[...], split_heads(k_v[...]), split_heads(v_v[...]), None)
    for h in range(HEADS):
        p_v[h] = probs[h]
    saves += fetch([(q_v, q_out), (k_v, k_out), (v_v, v_out), (p_v, p_out)], out_sem.at[pl.ds(0, 4)])
    copies[6].wait()
    branch = dot(attended, o_v[...])
    x1_v[...] = (tokens_v[...].astype(F32) + mod_v[0, 2, 0:1, :] * branch).astype(BF16).reshape(FRAMES, 2, D)
    saves += fetch([(x1_v, x1)], out_sem.at[pl.ds(4, 1)])
    wait_all(saves)


def spatial_attention_back_kernel(
    grad, mod, out_w, q_in, k_in, v_in, p_in, result, o_v, q_v, k_v, v_v, p_v, sems
):
    copies = fetch([(out_w.at[0], o_v), (v_in, v_v), (p_in, p_v), (k_in, k_v), (q_in, q_v)], sems)
    g = grad[...].reshape(TOK, D).astype(F32)
    branch_grad = (mod[0, 2, 0:1, :] * g).astype(BF16)
    wait_all(copies)
    attended_grad = dot(branch_grad, o_v[...], NT).astype(BF16)
    probs = [p_v[h] for h in range(HEADS)]
    grads = attend_back(probs, attended_grad, q_v[...], split_heads(k_v[...]), split_heads(v_v[...]))
    result[...] = lanes_of(grads).astype(BF16)


def spatial_input_back_kernel(grad, tokens, mod, qkv_w, projected_grad, result, tokens_v, w_v, result_v, sems):
    copies = fetch([(tokens, tokens_v), (qkv_w.at[0], w_v)], sems.at[pl.ds(0, 2)])
    copies[0].wait()
    g = grad[...].reshape(TOK, D).astype(F32)
    unit, inverse = layer_norm(tokens_v[...].astype(F32))
    copies[1].wait()
    normed_grad = dot(projected_grad[...], w_v[...]).astype(BF16).astype(F32)
    x_grad = layer_norm_back(normed_grad * (1.0 + mod[0, 1, 0:1, :]), unit, inverse)
    result_v[...] = (g + x_grad).astype(BF16)
    wait_all(fetch([(result_v, result)], sems.at[pl.ds(2, 1)]))


def temporal_normed_kernel(located, mod, sent, grouped_out, kept, unit_out, inverse_out, sem):
    unit, inverse = layer_norm(located[...].reshape(TOK, D).astype(F32))
    normed = (unit * (1.0 + mod[0, 1, 1:2, :]) + mod[0, 0, 1:2, :]).astype(BF16)
    grouped = regroup(normed)
    grouped_out[...] = rows_of([grouped[:, t * TOK : (t + 1) * TOK] for t in range(D // TOK)])
    save = pltpu.make_async_copy(grouped_out, sent, sem)
    save.start()
    kept[...] = normed
    unit_out[...] = unit
    inverse_out[...] = jnp.broadcast_to(inverse, (TOK, TOK))
    save.wait()


def temporal_attention_kernel(
    place, normed, grouped, cosines, sines, qkv_w, out_w, branch_grad,
    attended_out, normed_grad, own, to_1, to_2, to_3,
    w_out, branch_v, o_v, cos_v, sin_v, qkv_v, factors_v, wide, in_sems, sems, factor_sems,
):
    pairs = [(qkv_w.at[1, pl.ds(i * HW, HW)], w_out.at[pl.ds(i * HW, HW)]) for i in range(3)]
    pairs += [(cosines, cos_v), (sines, sin_v), (out_w.at[1], o_v), (branch_grad, branch_v)]
    copies = fetch(pairs, in_sems)
    messages = (own, to_1, to_2, to_3)
    saves = fetch([(grouped, ref.at[pl.ds(FACTOR[0], D)]) for ref in (own, to_1, to_3)], sems)
    for i in range(3):
        copies[i].wait()

        @pl.when(place[0] >= 0)
        def _(i=i):
            qkv_v[i] = dot(normed[...], w_out[i * HW : (i + 1) * HW, :], NT).astype(BF16)

    parts = [qkv_v[i] for i in range(3)]
    wait_all(copies[3:5])
    cos, sin = cos_v[...], sin_v[...]

    def rotate(t):
        t = t.astype(F32)
        return (t * cos + swap_halves(t) * sin).astype(BF16)

    def rotate_back(t):
        t = t.astype(BF16).astype(F32)
        return t * cos + swap_halves(t * sin)

    q, k, v = rotate(parts[0]), rotate(parts[1]), parts[2]
    keys_by_head, values_by_head = split_heads(k), split_heads(v)
    row = lax.broadcasted_iota(jnp.int32, (TOK, TOK), 0)
    column = lax.broadcasted_iota(jnp.int32, (TOK, TOK), 1)
    same = lax.rem(row, 2) == lax.rem(column, 2)
    probs, attended = attend(q, keys_by_head, values_by_head, same)
    attended_out[...] = attended
    wait_all(copies[5:])
    attended_grad = dot(branch_v[...], o_v[...], NT).astype(BF16)
    q_grad, k_grad, v_grad = attend_back(probs, attended_grad, q, keys_by_head, values_by_head)
    grads = lanes_of([rotate_back(q_grad), rotate_back(k_grad), v_grad])

    wide[: 3 * HW, :] = grads.T
    wide[3 * HW :, :] = attended.astype(F32).T
    empty = jnp.zeros((BLOCK - QKV_COLS - PROJ_ROWS, TOK), F32)
    for y in range(Y):
        pieces = []
        for s in range(PARTS):
            i = y * PARTS + s
            pieces += [
                wide[pl.ds(i * QKV_COLS, QKV_COLS), :],
                wide[pl.ds(3 * HW + i * PROJ_ROWS, PROJ_ROWS), :],
                empty,
            ]
        factors_v[y] = jnp.concatenate(pieces, axis=0).astype(BF16)
    saves += fetch(
        [(factors_v.at[lax.rem(place[0] + k, Y)], ref.at[pl.ds(0, FACTOR[0])]) for k, ref in enumerate(messages)],
        factor_sems,
    )
    normed_grad[...] = dot(grads.astype(BF16), w_out[...]).astype(BF16)
    wait_all(saves)


def temporal_input_back_kernel(normed_grad, seed, mod, unit, inverse, result, result_v, sem):
    g = seed[...].reshape(TOK, D).astype(F32)
    x_grad = layer_norm_back(normed_grad[...].astype(F32) * (1.0 + mod[0, 1, 1:2, :]), unit[...], inverse[:, 0:1])
    result_v[...] = (g + x_grad).astype(BF16).reshape(FRAMES, 2, D)
    save = pltpu.make_async_copy(result_v, result, sem)
    save.start()
    save.wait()


def block_out_kernel(attended, out_w, located, mod, result, o_v, located_v, result_v, sems):
    copies = fetch([(out_w.at[1], o_v), (located, located_v)], sems.at[pl.ds(0, 2)])
    wait_all(copies)
    x = located_v[...].reshape(TOK, D).astype(F32)
    branch = dot(attended[...], o_v[...])
    result_v[...] = (x + mod[0, 2, 1:2, :] * branch).astype(BF16).reshape(FRAMES, 2, D)
    wait_all(fetch([(result_v, result)], sems.at[pl.ds(2, 1)]))


def weight_grad_kernel(core, *refs):
    messages, branch_grad, normed_far = refs[0:Y], refs[Y : 2 * Y], refs[2 * Y]
    keep, *sends = refs[2 * Y + 1 : 2 * Y + 2 + PIECES]
    keep_v, send_v, sems = refs[2 * Y + 2 + PIECES :]
    left = lanes_of([m[: FACTOR[0]] for m in messages])
    normed = []
    for k, m in enumerate(messages):
        ref, at = (normed_far, 0) if k == 2 else (m, FACTOR[0])
        normed.append(lanes_of([ref[at + t * TOK : at + (t + 1) * TOK] for t in range(D // TOK)]))
    is_qkv = lax.rem(lax.broadcasted_iota(jnp.int32, (PARTS * BLOCK, 1), 0), BLOCK) < QKV_COLS
    from_normed = dot(left, rows_of(normed))
    from_branch = dot(left, rows_of([n[...] for n in branch_grad]))
    sums = jnp.where(is_qkv, from_normed, from_branch)
    tails = sums[:, 1024:].reshape(PARTS, 5, 8, TOK)
    first = core[0] == 0
    copies = []

    def chunk(d):
        main = [sums[:, d * 256 + i * TOK : d * 256 + (i + 1) * TOK].reshape(PARTS, BLOCK, TOK) for i in range(2)]
        packed = jnp.concatenate([tails[:, i, :, d * 32 : (d + 1) * 32] for i in range(4)], axis=-1)
        last = tails[:, 4]
        if d > 0:
            last = jnp.concatenate([last[:, :, d * 32 :], last[:, :, : d * 32]], axis=-1)
        rest = [m[:, 32:36] for m in main]
        whole_chunk = jnp.concatenate([m[:, :32] for m in main] + rest + [packed, last], axis=1)
        return whole_chunk.reshape(FLAT)

    for x in range(2):
        a, b = chunk(2 * x), chunk(2 * x + 1)
        send_v[x] = jnp.where(first, b, a).astype(BF16)
        keep_v[x] = jnp.where(first, a, b).astype(BF16)
        each = PIECES // 2
        pairs = [(send_v.at[x, pl.ds(i * PIECE[0], PIECE[0])], sends[x * each + i]) for i in range(each)]
        copies += fetch(pairs + [(keep_v.at[x], keep.at[x])], sems.at[x])
    wait_all(copies)


def load_kernel(*refs):
    half = len(refs) // 2
    wait_all(fetch(list(zip(refs[:half], refs[half : 2 * half], strict=True)), refs[-1]))


def add_kernel(kept, *refs):
    received, (result, result_v, sems) = refs[:PIECES], refs[PIECES:]
    copies = []
    for i, piece in enumerate(received):
        half, rows = i // (PIECES // 2), pl.ds(i % (PIECES // 2) * PIECE[0], PIECE[0])
        result_v[half, rows] = (kept[half, rows].astype(F32) + piece[...].astype(F32)).astype(BF16)
        if i % (PIECES // 2) == PIECES // 2 - 1:
            copies += fetch([(result_v.at[half], result.at[half])], sems.at[pl.ds(half, 1)])
    wait_all(copies)


def sum_kernel(parts, qkv, proj, qkv_v, proj_v, sems):
    total = parts[0].astype(F32)
    for i in range(1, 2 * PARTS):
        total = total + parts[i].astype(F32)
    packed, last = total[72:80], total[80:88]
    tail = jnp.concatenate([packed[:, i * 32 : (i + 1) * 32] for i in range(4)] + [last[:4, :32]], axis=0)
    main = [jnp.concatenate([total[:32], total[64:68]], axis=0), jnp.concatenate([total[32:64], total[68:72]], axis=0)]
    full = jnp.concatenate(main + [tail], axis=1)
    qkv_v[...] = full[:QKV_COLS]
    proj_v[...] = full[QKV_COLS : QKV_COLS + PROJ_ROWS]
    wait_all(fetch([(qkv_v, qkv), (proj_v, proj)], sems))


def call(kernel, name, inputs, outputs, scratch=(), mib=24, us=2.0):
    return pl.pallas_call(
        kernel,
        out_shape=tuple(space(shape, dtype) for space, dtype, shape in outputs),
        in_specs=[pl.BlockSpec(memory_space=space) for space, _ in inputs],
        out_specs=tuple(pl.BlockSpec(memory_space=space) for space, _, _ in outputs),
        scratch_shapes=list(scratch),
        compiler_params=pltpu.CompilerParams(vmem_limit_bytes=mib * 2**20),
        cost_estimate=pl.CostEstimate(flops=int(us * 1e9), bytes_accessed=int(us * 3e6), transcendentals=0),
        name=name,
    )(*[pltpu.with_memory_space_constraint(x, space) if space is not pltpu.SMEM else x for space, x in inputs])


def over(axis, size, k, x):
    return lax.ppermute(x, axis, [(i, (i + k) % size) for i in range(size)])


def hbm(n):
    return [pl.BlockSpec(memory_space=pltpu.HBM)] * n


def vmem(n):
    return [pl.BlockSpec(memory_space=pltpu.VMEM)] * n


def whole(*shape):
    return pl.BlockSpec(shape, lambda i: (0,) * len(shape))


def params(mib):
    return pltpu.CompilerParams(vmem_limit_bytes=mib * 2**20)


def out(dtype, *shape):
    return pltpu.HBM(shape, dtype)


def buf(dtype, *shape):
    return pltpu.VMEM(shape, dtype)


def dma(*n):
    return pltpu.SemaphoreType.DMA(n) if n else pltpu.SemaphoreType.DMA


HBM, VMEM, SMEM = pltpu.HBM, pltpu.VMEM, pltpu.SMEM
PAIRS = (FRAMES, 2, D)
MOD = (1, 3, 2, D)
QKV_W = (3 * HW, D)
OUT_W = (HW, D)
ATT = (TOK, HW)
PROB = (HEADS, TOK, TOK)
CHUNK = (88, TOK)
FLAT = (PARTS * 88, TOK)
PIECES = 2
PIECE = (2 * FLAT[0] // PIECES, TOK)
FACTOR = (PARTS * BLOCK, TOK)
MESSAGE = (FACTOR[0] + D, TOK)


def shards(tokens, modulation, frame_pos, qkv_weight, out_weight, seed_grad):
    seed = seed_grad.reshape(PAIRS)
    tokens = tokens.reshape(TOK, D)
    mod = modulation.transpose(0, 2, 1, 3)
    qkv_w = qkv_weight.swapaxes(1, 2)
    seq = ("y", "xl", "z")

    place = lax.axis_index("y").reshape(1).astype(jnp.int32)
    x1, q, k, v, p, sent, branch_grad = call(
        spatial_forward_kernel,
        "spatial_forward",
        [(SMEM, place), (HBM, tokens), (HBM, mod), (HBM, qkv_w), (HBM, out_weight), (HBM, seed)],
        [
            (HBM, BF16, PAIRS), (HBM, BF16, ATT), (HBM, BF16, ATT), (HBM, BF16, ATT), (HBM, BF16, PROB),
            (HBM, BF16, (TOK, D)), (HBM, BF16, (TOK, D)),
        ],
        [
            buf(BF16, *PAIRS), buf(BF16, TOK, D), buf(BF16, TOK, D), buf(BF16, TOK, D), buf(F32, *MOD), buf(BF16, *QKV_W), buf(BF16, *OUT_W), buf(BF16, TOK, D),
            buf(BF16, *PAIRS), buf(BF16, *ATT), buf(BF16, *ATT), buf(BF16, *ATT), buf(BF16, *PROB), dma(7), dma(7),
        ],
        us=5.0,
    )
    located = lax.all_to_all(x1, seq, split_axis=0, concat_axis=0, tiled=True)

    later_pos, _ = lax.optimization_barrier((frame_pos, x1))
    cosines, sines = call(
        tables_kernel,
        "tables",
        [(VMEM, later_pos.reshape(1, FRAMES))],
        [(HBM, F32, ATT), (HBM, F32, ATT)],
        [buf(F32, *ATT), buf(F32, *ATT), dma(2)],
        us=1.5,
    )
    branch_all = [sent] + [over("y", Y, i, sent) for i in range(1, Y)]

    located, branch_grad, cosines = lax.optimization_barrier((located, branch_grad, cosines))
    normed, grouped, normed_here, unit, inverse = call(
        temporal_normed_kernel,
        "temporal_normed",
        [(VMEM, located), (VMEM, mod)],
        [
            (HBM, BF16, (D, TOK)), (VMEM, BF16, (D, TOK)), (VMEM, BF16, (TOK, D)), (VMEM, F32, (TOK, D)),
            (VMEM, F32, (TOK, TOK)),
        ],
        [dma()],
        us=1.5,
    )
    normed_far = over("y", Y, 2, normed)

    attended, normed_grad, *messages = call(
        temporal_attention_kernel,
        "temporal_attention",
        [
            (SMEM, place), (VMEM, normed_here), (VMEM, grouped), (HBM, cosines), (HBM, sines), (HBM, qkv_w),
            (HBM, out_weight), (HBM, branch_grad),
        ],
        [(VMEM, BF16, ATT), (VMEM, BF16, (TOK, D))]
        + [(HBM, BF16, shape) for shape in (MESSAGE, MESSAGE, FACTOR, MESSAGE)],
        [
            buf(BF16, *QKV_W), buf(BF16, TOK, D), buf(BF16, *OUT_W), buf(F32, *ATT), buf(F32, *ATT), buf(BF16, 3, *ATT),
            buf(BF16, Y, *FACTOR), buf(F32, 4 * HW, TOK), dma(7), dma(3), dma(Y),
        ],
        us=7.0,
    )
    messages = [messages[0]] + [over("y", Y, i, messages[i]) for i in range(1, Y)]
    normed_grad, branch_all, normed_far = lax.optimization_barrier((normed_grad, branch_all, normed_far))
    (located_grad,) = call(
        temporal_input_back_kernel,
        "temporal_input_back",
        [(VMEM, normed_grad), (VMEM, seed), (VMEM, mod), (VMEM, unit), (VMEM, inverse)],
        [(HBM, BF16, PAIRS)],
        [buf(BF16, *PAIRS), dma()],
        us=3.0,
    )
    framed_grad = lax.all_to_all(located_grad, seq, split_axis=0, concat_axis=0, tiled=True)

    own_message, own_branch, _ = lax.optimization_barrier((messages[0], branch_all[0], located_grad))
    own_message, own_branch = call(
        load_kernel,
        "load_own",
        [(HBM, own_message), (HBM, own_branch)],
        [(VMEM, BF16, MESSAGE), (VMEM, BF16, (TOK, D))],
        [dma(2)],
        us=1.0,
    )
    messages, branch_all = [own_message] + messages[1:], [own_branch] + branch_all[1:]
    core = lax.axis_index("core").reshape(1).astype(jnp.int32)
    keep, *sends = call(
        weight_grad_kernel,
        "weight_grad",
        [(SMEM, core)] + [(VMEM, x) for x in (*messages, *branch_all, normed_far)],
        [(HBM, BF16, (2, *FLAT))] + [(HBM, BF16, PIECE)] * PIECES,
        [buf(BF16, 2, *FLAT), buf(BF16, 2, *FLAT), dma(2, 1 + PIECES // 2)],
        us=4.6,
    )
    swap = [(0, 1), (1, 0)]
    received = [lax.ppermute(send, "core", swap) for send in sends]

    (kept,) = call(
        load_kernel, "load", [(HBM, keep)], [(VMEM, BF16, (2, *FLAT))], [dma(1)], us=1.0
    )
    (halves,) = call(
        add_kernel,
        "add_cores",
        [(VMEM, kept)] + [(VMEM, x) for x in received],
        [(HBM, BF16, (2, *FLAT))],
        [buf(BF16, 2, *FLAT), dma(2)],
        us=1.0,
    )
    framed_grad, halves = lax.optimization_barrier((framed_grad, halves))
    parts = lax.all_to_all(
        halves.reshape(2 * PARTS, *CHUNK), ("xh", "xl", "z"), split_axis=0, concat_axis=0, tiled=True
    )

    framed_grad, attended, _ = lax.optimization_barrier((framed_grad, attended, halves))
    (projected_grad,) = call(
        spatial_attention_back_kernel,
        "spatial_attention_back",
        [(VMEM, framed_grad), (VMEM, mod), (HBM, out_weight), (HBM, q), (HBM, k), (HBM, v), (HBM, p)],
        [(VMEM, BF16, (TOK, 3 * HW))],
        [buf(BF16, *OUT_W), buf(BF16, *ATT), buf(BF16, *ATT), buf(BF16, *ATT), buf(BF16, *PROB), dma(5)],
        us=3.5,
    )
    (tokens_grad,) = call(
        spatial_input_back_kernel,
        "spatial_input_back",
        [(VMEM, framed_grad), (HBM, tokens), (VMEM, mod), (HBM, qkv_w), (VMEM, projected_grad)],
        [(HBM, BF16, (TOK, D))],
        [buf(BF16, TOK, D), buf(BF16, *QKV_W), buf(BF16, TOK, D), dma(3)],
        us=3.0,
    )
    (block_out,) = call(
        block_out_kernel,
        "block_out",
        [(VMEM, attended), (HBM, out_weight), (HBM, located), (VMEM, mod)],
        [(HBM, BF16, PAIRS)],
        [buf(BF16, *OUT_W), buf(BF16, *PAIRS), buf(BF16, *PAIRS), dma(3)],
        us=2.0,
    )
    qkv_grad, proj_grad = call(
        sum_kernel,
        "sum_parts",
        [(VMEM, parts)],
        [(HBM, F32, (QKV_COLS, WIDTH)), (HBM, F32, (PROJ_ROWS, WIDTH))],
        [buf(F32, QKV_COLS, WIDTH), buf(F32, PROJ_ROWS, WIDTH), dma(2)],
        us=1.5,
    )
    return (
        block_out.reshape(1, FRAMES, 2, D),
        tokens_grad.reshape(1, 1, LOC, D),
        qkv_grad.T,
        proj_grad,
    )


def solution(mesh):
    sizes = (2, 2, 4, 2, 8)
    split = Mesh(mesh.devices.reshape(sizes), ("xh", "core", "y", "xl", "z"))
    dp, seq = ("xh", "core"), ("y", "xl", "z")
    return jax.shard_map(
        shards,
        mesh=split,
        in_specs=(
            P(dp, seq, None, None),
            P(dp, None, None, None),
            P(),
            P(),
            P(),
            P(dp, None, seq, None),
        ),
        out_specs=(
            P(dp, None, seq, None),
            P(dp, seq, None, None),
            P(dp, seq),
            P(seq, dp),
        ),
        check_vma=False,
    )
```

```python
from functools import partial
import math

import jax
import jax.numpy as jnp
import numpy as np
from jax import lax
from jax.experimental import pallas as pl
from jax.experimental.pallas import tpu as pltpu
from jax.sharding import Mesh, PartitionSpec as P

D = 1152
HEADS = 8
HEAD_DIM = 72
HALF = HEAD_DIM // 2
HW = 576
LOC = 128
FRAMES = 64
TOK = 128
SCALE = HEAD_DIM ** (-0.5)
EPS = 1e-06
ROPE_BASE = 10000.0
QKV_COLS = 27
PROJ_ROWS = 9
BLOCK = 40
Y = 4
PARTS = 16
WIDTH = D // 4
F32 = jnp.float32
BF16 = jnp.bfloat16

NN = (((1,), (0,)), ((), ()))
NT = (((1,), (1,)), ((), ()))
TN = (((0,), (0,)), ((), ()))


def dot(a, b, dims=NN):
    return lax.dot_general(a, b, dims, preferred_element_type=F32)


def layer_norm(x):
    centered = x - jnp.mean(x, axis=-1, keepdims=True)
    inverse = lax.rsqrt(jnp.mean(centered * centered, axis=-1, keepdims=True) + EPS)
    return centered * inverse, inverse


def layer_norm_back(grad, unit, inverse):
    first = jnp.mean(grad, axis=-1, keepdims=True)
    second = jnp.mean(grad * unit, axis=-1, keepdims=True)
    return inverse * (grad - first - unit * second)


def split_heads(x):
    lane = lax.broadcasted_iota(jnp.int32, (1, HW), 1)
    parts = []
    for h in range(HEADS):
        mine = ((lane >= h * HEAD_DIM) & (lane < (h + 1) * HEAD_DIM)).astype(F32).astype(BF16)
        parts.append(x * mine)
    return jnp.concatenate(parts, axis=0)


def head(x, h):
    return x[:, h * TOK : (h + 1) * TOK]


def rows_of(parts):
    return jnp.concatenate(parts, axis=0)


def lanes_of(parts):
    return jnp.concatenate(parts, axis=1)


def attend(query, keys_by_head, values_by_head, allowed):
    scores = dot(query, keys_by_head, NT)
    probs = []
    for h in range(HEADS):
        s = head(scores, h) * SCALE
        if allowed is not None:
            s = jnp.where(allowed, s, -1e30)
        e = jnp.exp(s - jnp.max(s, axis=-1, keepdims=True))
        probs.append((e / jnp.sum(e, axis=-1, keepdims=True)).astype(BF16))
    return probs, dot(lanes_of(probs), values_by_head).astype(BF16)


def attend_back(probs, attended_grad, query, keys_by_head, values_by_head):
    prob_grads = dot(attended_grad, values_by_head, NT)
    values_grad = dot(rows_of(probs), split_heads(attended_grad), TN)
    score_grads = []
    for h in range(HEADS):
        p = probs[h].astype(F32)
        g = head(prob_grads, h)
        s = p * (g - jnp.sum(g * p, axis=-1, keepdims=True)) * SCALE
        score_grads.append(s.astype(BF16))
    query_grad = dot(lanes_of(score_grads), keys_by_head)
    keys_grad = dot(rows_of(score_grads), split_heads(query), TN)
    return query_grad, keys_grad, values_grad


def swap_halves(x):
    lane = lax.broadcasted_iota(jnp.int32, (1, HW), 1)
    first = lax.rem(lane, HEAD_DIM) < HALF
    later = jnp.concatenate([x[:, HALF:], x[:, :HALF]], axis=1)
    earlier = jnp.concatenate([x[:, HW - HALF :], x[:, : HW - HALF]], axis=1)
    return jnp.where(first, later, earlier)


def fetch(pairs, sems):
    copies = [pltpu.make_async_copy(src, dst, sems.at[i]) for i, (src, dst) in enumerate(pairs)]
    for c in copies:
        c.start()
    return copies


def store(pairs, sems):
    return fetch(pairs, sems)


def start_all(copies):
    for c in copies:
        c.start()


def wait_all(copies):
    for c in copies:
        c.wait()


def regroup(x):
    main = [x[:, d * WIDTH : d * WIDTH + 256] for d in range(4)]
    tail = [x[:, d * WIDTH + 256 : (d + 1) * WIDTH] for d in range(4)]
    return jnp.concatenate(main + tail, axis=1)


def rope_tables(pos):
    row = lax.broadcasted_iota(jnp.int32, (TOK, FRAMES), 0)
    frame = lax.broadcasted_iota(jnp.int32, (TOK, FRAMES), 1)
    mine = (row >= 2 * frame) & (row < 2 * frame + 2)
    time = jnp.sum(jnp.where(mine, pos.astype(F32), 0.0), axis=-1, keepdims=True)
    lane = lax.broadcasted_iota(jnp.int32, (1, HW), 1)
    frequency = jnp.exp(lax.rem(lane, HALF).astype(F32) * (-2.0 * math.log(ROPE_BASE) / HEAD_DIM))
    angles = time * frequency
    sign = jnp.where(lax.rem(lane, HEAD_DIM) < HALF, -1.0, 1.0)
    return jnp.cos(angles), jnp.sin(angles) * sign


def tables_kernel(pos, cos_out, sin_out, cos_v, sin_v, sems):
    cos_v[...], sin_v[...] = rope_tables(pos[...])
    wait_all(fetch([(cos_v, cos_out), (sin_v, sin_out)], sems))


def spatial_forward_kernel(
    place, tokens, mod, qkv_w, out_w, seed, x1, q_out, k_out, v_out, p_out, sent, kept,
    seed_v, sent_v, kept_v, tokens_v, mod_v, w_v, o_v, normed_v, x1_v, q_v, k_v, v_v, p_v, in_sem, out_sem,
):
    pairs = [(tokens, tokens_v), (mod, mod_v), (seed, seed_v)]
    pairs += [(qkv_w.at[0, pl.ds(i * HW, HW)], w_v.at[pl.ds(i * HW, HW)]) for i in range(3)] + [(out_w.at[0], o_v)]
    copies = [pltpu.make_async_copy(src, dst, in_sem.at[i]) for i, (src, dst) in enumerate(pairs)]
    start_all(copies)
    wait_all(copies[:3])

    @pl.when(place[0] >= 0)
    def _():
        unit, _ = layer_norm(tokens_v[...].astype(F32))
        normed_v[...] = (unit * (1.0 + mod_v[0, 1, 0:1, :]) + mod_v[0, 0, 0:1, :]).astype(BF16)
        branch_grad = (mod_v[0, 2, 1:2, :] * seed_v[...].reshape(TOK, D).astype(F32)).astype(BF16)
        sent_v[...] = regroup(branch_grad)
        kept_v[...] = branch_grad

    saves = fetch([(sent_v, sent), (kept_v, kept)], out_sem.at[pl.ds(5, 2)])

    for i, held in enumerate((q_v, k_v, v_v)):
        copies[3 + i].wait()

        @pl.when(place[0] >= 0)
        def _(i=i, held=held):
            held[...] = dot(normed_v[...], w_v[i * HW : (i + 1) * HW, :], NT).astype(BF16)

    probs, attended = attend(q_v[...], split_heads(k_v[...]), split_heads(v_v[...]), None)
    for h in range(HEADS):
        p_v[h] = probs[h]
    saves += fetch([(q_v, q_out), (k_v, k_out), (v_v, v_out), (p_v, p_out)], out_sem.at[pl.ds(0, 4)])
    copies[6].wait()
    branch = dot(attended, o_v[...])
    x1_v[...] = (tokens_v[...].astype(F32) + mod_v[0, 2, 0:1, :] * branch).astype(BF16).reshape(FRAMES, 2, D)
    saves += fetch([(x1_v, x1)], out_sem.at[pl.ds(4, 1)])
    wait_all(saves)


def spatial_attention_back_kernel(
    grad, mod, out_w, q_in, k_in, v_in, p_in, result, o_v, q_v, k_v, v_v, p_v, sems
):
    copies = fetch([(out_w.at[0], o_v), (v_in, v_v), (p_in, p_v), (k_in, k_v), (q_in, q_v)], sems)
    g = grad[...].reshape(TOK, D).astype(F32)
    branch_grad = (mod[0, 2, 0:1, :] * g).astype(BF16)
    wait_all(copies)
    attended_grad = dot(branch_grad, o_v[...], NT).astype(BF16)
    probs = [p_v[h] for h in range(HEADS)]
    grads = attend_back(probs, attended_grad, q_v[...], split_heads(k_v[...]), split_heads(v_v[...]))
    result[...] = lanes_of(grads).astype(BF16)


def spatial_input_back_kernel(grad, tokens, mod, qkv_w, projected_grad, result, tokens_v, w_v, result_v, sems):
    copies = fetch([(tokens, tokens_v), (qkv_w.at[0], w_v)], sems.at[pl.ds(0, 2)])
    copies[0].wait()
    g = grad[...].reshape(TOK, D).astype(F32)
    unit, inverse = layer_norm(tokens_v[...].astype(F32))
    copies[1].wait()
    normed_grad = dot(projected_grad[...], w_v[...]).astype(BF16).astype(F32)
    x_grad = layer_norm_back(normed_grad * (1.0 + mod[0, 1, 0:1, :]), unit, inverse)
    result_v[...] = (g + x_grad).astype(BF16)
    wait_all(fetch([(result_v, result)], sems.at[pl.ds(2, 1)]))


def temporal_normed_kernel(located, mod, sent, grouped_out, kept, unit_out, inverse_out, sem):
    unit, inverse = layer_norm(located[...].reshape(TOK, D).astype(F32))
    normed = (unit * (1.0 + mod[0, 1, 1:2, :]) + mod[0, 0, 1:2, :]).astype(BF16)
    grouped = regroup(normed)
    grouped_out[...] = rows_of([grouped[:, t * TOK : (t + 1) * TOK] for t in range(D // TOK)])
    save = pltpu.make_async_copy(grouped_out, sent, sem)
    save.start()
    kept[...] = normed
    unit_out[...] = unit.astype(BF16)
    inverse_out[...] = jnp.broadcast_to(inverse, (TOK, TOK))
    save.wait()


def temporal_attention_kernel(
    place, normed, grouped, cosines, sines, qkv_w, out_w, branch_grad,
    attended_out, normed_grad, own, to_1, to_2, to_3,
    w_out, branch_v, o_v, cos_v, sin_v, qkv_v, factors_v, wide, in_sems, sems, factor_sems,
):
    pairs = [(qkv_w.at[1, pl.ds(i * HW, HW)], w_out.at[pl.ds(i * HW, HW)]) for i in range(3)]
    pairs += [(cosines, cos_v), (sines, sin_v), (out_w.at[1], o_v), (branch_grad, branch_v)]
    copies = fetch(pairs, in_sems)
    messages = (own, to_1, to_2, to_3)
    saves = fetch([(grouped, ref.at[pl.ds(FACTOR[0], D)]) for ref in (own, to_1, to_3)], sems)
    for i in range(3):
        copies[i].wait()

        @pl.when(place[0] >= 0)
        def _(i=i):
            qkv_v[i] = dot(normed[...], w_out[i * HW : (i + 1) * HW, :], NT).astype(BF16)

    parts = [qkv_v[i] for i in range(3)]
    wait_all(copies[3:5])
    cos, sin = cos_v[...], sin_v[...]

    def rotate(t):
        t = t.astype(F32)
        return (t * cos + swap_halves(t) * sin).astype(BF16)

    def rotate_back(t):
        t = t.astype(BF16).astype(F32)
        return t * cos + swap_halves(t * sin)

    q, k, v = rotate(parts[0]), rotate(parts[1]), parts[2]
    keys_by_head, values_by_head = split_heads(k), split_heads(v)
    row = lax.broadcasted_iota(jnp.int32, (TOK, TOK), 0)
    column = lax.broadcasted_iota(jnp.int32, (TOK, TOK), 1)
    same = lax.rem(row, 2) == lax.rem(column, 2)
    probs, attended = attend(q, keys_by_head, values_by_head, same)
    attended_out[...] = attended
    wait_all(copies[5:])
    attended_grad = dot(branch_v[...], o_v[...], NT).astype(BF16)
    q_grad, k_grad, v_grad = attend_back(probs, attended_grad, q, keys_by_head, values_by_head)
    grads = lanes_of([rotate_back(q_grad), rotate_back(k_grad), v_grad])

    wide[: 3 * HW, :] = grads.T
    wide[3 * HW :, :] = attended.astype(F32).T
    empty = jnp.zeros((BLOCK - QKV_COLS - PROJ_ROWS, TOK), F32)
    for y in range(Y):
        pieces = []
        for s in range(PARTS):
            i = y * PARTS + s
            pieces += [
                wide[pl.ds(i * QKV_COLS, QKV_COLS), :],
                wide[pl.ds(3 * HW + i * PROJ_ROWS, PROJ_ROWS), :],
                empty,
            ]
        factors_v[y] = jnp.concatenate(pieces, axis=0).astype(BF16)
    saves += fetch(
        [(factors_v.at[lax.rem(place[0] + k, Y)], ref.at[pl.ds(0, FACTOR[0])]) for k, ref in enumerate(messages)],
        factor_sems,
    )
    normed_grad[...] = dot(grads.astype(BF16), w_out[...]).astype(BF16)
    wait_all(saves)


def temporal_input_back_kernel(normed_grad, seed, mod, unit, inverse, result, result_v, sem):
    g = seed[...].reshape(TOK, D).astype(F32)
    x_grad = layer_norm_back(normed_grad[...].astype(F32) * (1.0 + mod[0, 1, 1:2, :]), unit[...].astype(F32), inverse[:, 0:1])
    result_v[...] = (g + x_grad).astype(BF16).reshape(FRAMES, 2, D)
    save = pltpu.make_async_copy(result_v, result, sem)
    save.start()
    save.wait()


def block_out_kernel(attended, out_w, located, mod, result, o_v, located_v, result_v, sems):
    copies = fetch([(out_w.at[1], o_v), (located, located_v)], sems.at[pl.ds(0, 2)])
    wait_all(copies)
    x = located_v[...].reshape(TOK, D).astype(F32)
    branch = dot(attended[...], o_v[...])
    result_v[...] = (x + mod[0, 2, 1:2, :] * branch).astype(BF16).reshape(FRAMES, 2, D)
    wait_all(fetch([(result_v, result)], sems.at[pl.ds(2, 1)]))


def weight_grad_kernel(core, *refs):
    messages, branch_grad, normed_far = refs[0:Y], refs[Y : 2 * Y], refs[2 * Y]
    keep, *sends = refs[2 * Y + 1 : 2 * Y + 2 + PIECES]
    keep_v, send_v, sems = refs[2 * Y + 2 + PIECES :]
    left = lanes_of([m[: FACTOR[0]] for m in messages])
    normed = []
    for k, m in enumerate(messages):
        ref, at = (normed_far, 0) if k == 2 else (m, FACTOR[0])
        normed.append(lanes_of([ref[at + t * TOK : at + (t + 1) * TOK] for t in range(D // TOK)]))
    is_qkv = lax.rem(lax.broadcasted_iota(jnp.int32, (PARTS * BLOCK, 1), 0), BLOCK) < QKV_COLS
    from_normed = dot(left, rows_of(normed))
    from_branch = dot(left, rows_of([n[...] for n in branch_grad]))
    sums = jnp.where(is_qkv, from_normed, from_branch)
    tails = sums[:, 1024:].reshape(PARTS, 5, 8, TOK)
    first = core[0] == 0
    copies = []

    def chunk(d):
        main = [sums[:, d * 256 + i * TOK : d * 256 + (i + 1) * TOK].reshape(PARTS, BLOCK, TOK) for i in range(2)]
        packed = jnp.concatenate([tails[:, i, :, d * 32 : (d + 1) * 32] for i in range(4)], axis=-1)
        last = tails[:, 4]
        if d > 0:
            last = jnp.concatenate([last[:, :, d * 32 :], last[:, :, : d * 32]], axis=-1)
        rest = [m[:, 32:36] for m in main]
        whole_chunk = jnp.concatenate([m[:, :32] for m in main] + rest + [packed, last], axis=1)
        return whole_chunk.reshape(FLAT)

    for x in range(2):
        a, b = chunk(2 * x), chunk(2 * x + 1)
        send_v[x] = jnp.where(first, b, a).astype(BF16)
        keep_v[x] = jnp.where(first, a, b).astype(BF16)
        each = PIECES // 2
        pairs = [(send_v.at[x, pl.ds(i * PIECE[0], PIECE[0])], sends[x * each + i]) for i in range(each)]
        copies += fetch(pairs + [(keep_v.at[x], keep.at[x])], sems.at[x])
    wait_all(copies)


def load_kernel(*refs):
    half = len(refs) // 2
    wait_all(fetch(list(zip(refs[:half], refs[half : 2 * half], strict=True)), refs[-1]))


def add_kernel(kept, *refs):
    received, (result, result_v, sems) = refs[:PIECES], refs[PIECES:]
    copies = []
    for i, piece in enumerate(received):
        half, rows = i // (PIECES // 2), pl.ds(i % (PIECES // 2) * PIECE[0], PIECE[0])
        result_v[half, rows] = (kept[half, rows].astype(F32) + piece[...].astype(F32)).astype(BF16)
        if i % (PIECES // 2) == PIECES // 2 - 1:
            copies += fetch([(result_v.at[half], result.at[half])], sems.at[pl.ds(half, 1)])
    wait_all(copies)


def sum_kernel(parts, qkv, proj, qkv_v, proj_v, sems):
    total = parts[0].astype(F32)
    for i in range(1, 2 * PARTS):
        total = total + parts[i].astype(F32)
    packed, last = total[72:80], total[80:88]
    tail = jnp.concatenate([packed[:, i * 32 : (i + 1) * 32] for i in range(4)] + [last[:4, :32]], axis=0)
    main = [jnp.concatenate([total[:32], total[64:68]], axis=0), jnp.concatenate([total[32:64], total[68:72]], axis=0)]
    full = jnp.concatenate(main + [tail], axis=1)
    qkv_v[...] = full[:QKV_COLS]
    proj_v[...] = full[QKV_COLS : QKV_COLS + PROJ_ROWS]
    wait_all(fetch([(qkv_v, qkv), (proj_v, proj)], sems))


def call(kernel, name, inputs, outputs, scratch=(), mib=24, us=2.0):
    return pl.pallas_call(
        kernel,
        out_shape=tuple(space(shape, dtype) for space, dtype, shape in outputs),
        in_specs=[pl.BlockSpec(memory_space=space) for space, _ in inputs],
        out_specs=tuple(pl.BlockSpec(memory_space=space) for space, _, _ in outputs),
        scratch_shapes=list(scratch),
        compiler_params=pltpu.CompilerParams(vmem_limit_bytes=mib * 2**20),
        cost_estimate=pl.CostEstimate(flops=int(us * 1e9), bytes_accessed=int(us * 3e6), transcendentals=0),
        name=name,
    )(*[pltpu.with_memory_space_constraint(x, space) if space is not pltpu.SMEM else x for space, x in inputs])


def over(axis, size, k, x):
    return lax.ppermute(x, axis, [(i, (i + k) % size) for i in range(size)])


def hbm(n):
    return [pl.BlockSpec(memory_space=pltpu.HBM)] * n


def vmem(n):
    return [pl.BlockSpec(memory_space=pltpu.VMEM)] * n


def whole(*shape):
    return pl.BlockSpec(shape, lambda i: (0,) * len(shape))


def params(mib):
    return pltpu.CompilerParams(vmem_limit_bytes=mib * 2**20)


def out(dtype, *shape):
    return pltpu.HBM(shape, dtype)


def buf(dtype, *shape):
    return pltpu.VMEM(shape, dtype)


def dma(*n):
    return pltpu.SemaphoreType.DMA(n) if n else pltpu.SemaphoreType.DMA


HBM, VMEM, SMEM = pltpu.HBM, pltpu.VMEM, pltpu.SMEM
PAIRS = (FRAMES, 2, D)
MOD = (1, 3, 2, D)
QKV_W = (3 * HW, D)
OUT_W = (HW, D)
ATT = (TOK, HW)
PROB = (HEADS, TOK, TOK)
CHUNK = (88, TOK)
FLAT = (PARTS * 88, TOK)
PIECES = 2
PIECE = (2 * FLAT[0] // PIECES, TOK)
FACTOR = (PARTS * BLOCK, TOK)
MESSAGE = (FACTOR[0] + D, TOK)


def shards(tokens, modulation, frame_pos, qkv_weight, out_weight, seed_grad):
    seed = seed_grad.reshape(PAIRS)
    tokens = tokens.reshape(TOK, D)
    mod = modulation.transpose(0, 2, 1, 3)
    qkv_w = qkv_weight.swapaxes(1, 2)
    seq = ("y", "xl", "z")

    place = lax.axis_index("y").reshape(1).astype(jnp.int32)
    x1, q, k, v, p, sent, branch_grad = call(
        spatial_forward_kernel,
        "spatial_forward",
        [(SMEM, place), (HBM, tokens), (HBM, mod), (HBM, qkv_w), (HBM, out_weight), (HBM, seed)],
        [
            (HBM, BF16, PAIRS), (HBM, BF16, ATT), (HBM, BF16, ATT), (HBM, BF16, ATT), (HBM, BF16, PROB),
            (HBM, BF16, (TOK, D)), (HBM, BF16, (TOK, D)),
        ],
        [
            buf(BF16, *PAIRS), buf(BF16, TOK, D), buf(BF16, TOK, D), buf(BF16, TOK, D), buf(F32, *MOD), buf(BF16, *QKV_W), buf(BF16, *OUT_W), buf(BF16, TOK, D),
            buf(BF16, *PAIRS), buf(BF16, *ATT), buf(BF16, *ATT), buf(BF16, *ATT), buf(BF16, *PROB), dma(7), dma(7),
        ],
        us=5.0,
    )
    located = lax.all_to_all(x1, seq, split_axis=0, concat_axis=0, tiled=True)

    later_pos, _ = lax.optimization_barrier((frame_pos, x1))
    cosines, sines = call(
        tables_kernel,
        "tables",
        [(VMEM, later_pos.reshape(1, FRAMES))],
        [(HBM, F32, ATT), (HBM, F32, ATT)],
        [buf(F32, *ATT), buf(F32, *ATT), dma(2)],
        us=1.5,
    )
    branch_all = [sent] + [over("y", Y, i, sent) for i in range(1, Y)]

    located, branch_grad, cosines = lax.optimization_barrier((located, branch_grad, cosines))
    normed, grouped, normed_here, unit, inverse = call(
        temporal_normed_kernel,
        "temporal_normed",
        [(VMEM, located), (VMEM, mod)],
        [
            (HBM, BF16, (D, TOK)), (VMEM, BF16, (D, TOK)), (VMEM, BF16, (TOK, D)), (VMEM, BF16, (TOK, D)),
            (VMEM, F32, (TOK, TOK)),
        ],
        [dma()],
        us=1.5,
    )
    normed_far = over("y", Y, 2, normed)

    attended, normed_grad, *messages = call(
        temporal_attention_kernel,
        "temporal_attention",
        [
            (SMEM, place), (VMEM, normed_here), (VMEM, grouped), (HBM, cosines), (HBM, sines), (HBM, qkv_w),
            (HBM, out_weight), (HBM, branch_grad),
        ],
        [(VMEM, BF16, ATT), (VMEM, BF16, (TOK, D))]
        + [(HBM, BF16, shape) for shape in (MESSAGE, MESSAGE, FACTOR, MESSAGE)],
        [
            buf(BF16, *QKV_W), buf(BF16, TOK, D), buf(BF16, *OUT_W), buf(F32, *ATT), buf(F32, *ATT), buf(BF16, 3, *ATT),
            buf(BF16, Y, *FACTOR), buf(F32, 4 * HW, TOK), dma(7), dma(3), dma(Y),
        ],
        us=7.0,
    )
    messages = [messages[0]] + [over("y", Y, i, messages[i]) for i in range(1, Y)]
    normed_grad, branch_all, normed_far = lax.optimization_barrier((normed_grad, branch_all, normed_far))
    (located_grad,) = call(
        temporal_input_back_kernel,
        "temporal_input_back",
        [(VMEM, normed_grad), (VMEM, seed), (VMEM, mod), (VMEM, unit), (VMEM, inverse)],
        [(HBM, BF16, PAIRS)],
        [buf(BF16, *PAIRS), dma()],
        us=3.0,
    )
    framed_grad = lax.all_to_all(located_grad, seq, split_axis=0, concat_axis=0, tiled=True)

    own_message, own_branch, _ = lax.optimization_barrier((messages[0], branch_all[0], located_grad))
    own_message, own_branch = call(
        load_kernel,
        "load_own",
        [(HBM, own_message), (HBM, own_branch)],
        [(VMEM, BF16, MESSAGE), (VMEM, BF16, (TOK, D))],
        [dma(2)],
        us=1.0,
    )
    messages, branch_all = [own_message] + messages[1:], [own_branch] + branch_all[1:]
    core = lax.axis_index("core").reshape(1).astype(jnp.int32)
    keep, *sends = call(
        weight_grad_kernel,
        "weight_grad",
        [(SMEM, core)] + [(VMEM, x) for x in (*messages, *branch_all, normed_far)],
        [(HBM, BF16, (2, *FLAT))] + [(HBM, BF16, PIECE)] * PIECES,
        [buf(BF16, 2, *FLAT), buf(BF16, 2, *FLAT), dma(2, 1 + PIECES // 2)],
        us=4.6,
    )
    swap = [(0, 1), (1, 0)]
    received = [lax.ppermute(send, "core", swap) for send in sends]

    (kept,) = call(
        load_kernel, "load", [(HBM, keep)], [(VMEM, BF16, (2, *FLAT))], [dma(1)], us=1.0
    )
    (halves,) = call(
        add_kernel,
        "add_cores",
        [(VMEM, kept)] + [(VMEM, x) for x in received],
        [(HBM, BF16, (2, *FLAT))],
        [buf(BF16, 2, *FLAT), dma(2)],
        us=1.0,
    )
    framed_grad, halves = lax.optimization_barrier((framed_grad, halves))
    parts = lax.all_to_all(
        halves.reshape(2 * PARTS, *CHUNK), ("xh", "xl", "z"), split_axis=0, concat_axis=0, tiled=True
    )

    framed_grad, attended, _ = lax.optimization_barrier((framed_grad, attended, halves))
    (projected_grad,) = call(
        spatial_attention_back_kernel,
        "spatial_attention_back",
        [(VMEM, framed_grad), (VMEM, mod), (HBM, out_weight), (HBM, q), (HBM, k), (HBM, v), (HBM, p)],
        [(VMEM, BF16, (TOK, 3 * HW))],
        [buf(BF16, *OUT_W), buf(BF16, *ATT), buf(BF16, *ATT), buf(BF16, *ATT), buf(BF16, *PROB), dma(5)],
        us=3.5,
    )
    (tokens_grad,) = call(
        spatial_input_back_kernel,
        "spatial_input_back",
        [(VMEM, framed_grad), (HBM, tokens), (VMEM, mod), (HBM, qkv_w), (VMEM, projected_grad)],
        [(HBM, BF16, (TOK, D))],
        [buf(BF16, TOK, D), buf(BF16, *QKV_W), buf(BF16, TOK, D), dma(3)],
        us=3.0,
    )
    (block_out,) = call(
        block_out_kernel,
        "block_out",
        [(VMEM, attended), (HBM, out_weight), (HBM, located), (VMEM, mod)],
        [(HBM, BF16, PAIRS)],
        [buf(BF16, *OUT_W), buf(BF16, *PAIRS), buf(BF16, *PAIRS), dma(3)],
        us=2.0,
    )
    qkv_grad, proj_grad = call(
        sum_kernel,
        "sum_parts",
        [(VMEM, parts)],
        [(HBM, F32, (QKV_COLS, WIDTH)), (HBM, F32, (PROJ_ROWS, WIDTH))],
        [buf(F32, QKV_COLS, WIDTH), buf(F32, PROJ_ROWS, WIDTH), dma(2)],
        us=1.5,
    )
    return (
        block_out.reshape(1, FRAMES, 2, D),
        tokens_grad.reshape(1, 1, LOC, D),
        qkv_grad.T,
        proj_grad,
    )


def solution(mesh):
    sizes = (2, 2, 4, 2, 8)
    split = Mesh(mesh.devices.reshape(sizes), ("xh", "core", "y", "xl", "z"))
    dp, seq = ("xh", "core"), ("y", "xl", "z")
    return jax.shard_map(
        shards,
        mesh=split,
        in_specs=(
            P(dp, seq, None, None),
            P(dp, None, None, None),
            P(),
            P(),
            P(),
            P(dp, None, seq, None),
        ),
        out_specs=(
            P(dp, None, seq, None),
            P(dp, seq, None, None),
            P(dp, seq),
            P(seq, dp),
        ),
        check_vma=False,
    )
```
